512 devices in a mesh: ta: 16 (over y_hi, z), gz: 8 (over y_lo, core), yx: 4 (over x).
Axes of the slice: x: 4, y: 8 (y_hi: 2, y_lo: 4; y = y_hi * 4 + y_lo), z: 8, core: 2. Of those that a mesh axis runs over, the one named last changes fastest.
Arguments:
- source: bfloat16 [16, 8, 4, 12, 32, 128], P('ta', 'gz', 'yx'), may hold values from -180 to 180
- diag_block: bfloat16 [16, 8, 4, 12, 128, 128], P('ta', 'gz', 'yx'), may hold values from -2 to 7
- link_time: bfloat16 [16, 8, 4, 12, 128, 128], P('ta', 'gz', 'yx'), may hold values from -0.25 to 0.25
- link_zaxis: bfloat16 [16, 8, 4, 12, 128, 128], P('ta', 'gz', 'yx'), may hold values from -0.25 to 0.25
- link_yaxis: bfloat16 [16, 8, 4, 12, 128, 128], P('ta', 'gz', 'yx'), may hold values from -0.25 to 0.25
- link_xaxis: bfloat16 [16, 8, 4, 12, 128, 128], P('ta', 'gz', 'yx'), may hold values from -0.25 to 0.25
- prolong: bfloat16 [16, 8, 4, 12, 128, 128], P('ta', 'gz', 'yx'), may hold values from -0.375 to 0.375
- top_diag: bfloat16 [16, 8, 4, 128, 128], P('ta', 'gz', 'yx'), may hold values from -0.5 to 0.5
- top_time: bfloat16 [16, 8, 4, 128, 128], P('ta', 'gz', 'yx'), may hold values from -0.25 to 0.25
- top_zaxis: bfloat16 [16, 8, 4, 128, 128], P('ta', 'gz', 'yx'), may hold values from -0.25 to 0.25
- top_yaxis: bfloat16 [16, 8, 4, 128, 128], P('ta', 'gz', 'yx'), may hold values from -0.25 to 0.25
Outputs:
- update: float32 [16, 8, 4, 12, 32, 128], P('ta', 'gz', 'yx')
- remainder: float32 [16, 8, 4, 12, 32, 128], P('ta', 'gz', 'yx')
The draws below stay inside these ranges and needn't reach their ends.
All inputs are finite; a program needn't handle non-finite values.
Results may differ from the reference program's by a relative error of at most 0.01.
Values may be sent and summed in bfloat16 or wider, within the bound.
A program may use at most 64 MiB of HBM per device.

```python
import math
import jax
import jax.numpy as jnp
from jax import lax

DOF = 128
DC = 128
RHS = 32
LT_DEV = 1
NX = 12
NT = 16
NZ = 8
NY = 4
N_TA = 16
N_GZ = 8
N_YX = 4


def draw_source(key, part):
    key = jax.random.fold_in(key, 11)
    first_key, second_key = jax.random.split(key, 2)
    shape_full = (NT, NZ, NY, NX, RHS, DOF)
    base = jnp.clip(jax.random.normal(first_key, shape_full, jnp.float32), -6.0, 6.0)
    column_scale = jnp.exp(jax.random.uniform(second_key, (RHS,), jnp.float32, 0.0, math.log(10.0)))
    slices = jnp.arange(NT).astype(jnp.float32) / max(NT - 1, 1)
    rising = 1.0 + 2.0 * slices
    scaled = base * rising[:, None, None, None, None, None] * column_scale[None, None, None, None, :, None]
    return scaled.astype(jnp.bfloat16)


def draw_diag_block(key, part):
    key = jax.random.fold_in(key, 23)
    noise_key, jitter_key = jax.random.split(key, 2)
    shape_full = (NT, NZ, NY, NX, DOF, DOF)
    spread = 1.0 / math.sqrt(DOF)
    noise = jnp.clip(jax.random.normal(noise_key, shape_full, jnp.float32), -6.0, 6.0) * spread
    level = jnp.arange(NT).astype(jnp.float32) / max(NT - 1, 1)
    mass_time = 0.5 * jnp.exp(level * math.log(8.0))
    jitter = jnp.exp(jax.random.uniform(jitter_key, (NT, NZ, NY, NX), jnp.float32, math.log(0.8), math.log(1.25)))
    mass = mass_time[:, None, None, None] * jitter
    identity = jnp.eye(DOF, dtype=jnp.float32)
    blocks = noise + mass[:, :, :, :, None, None] * identity[None, None, None, None]
    return blocks.astype(jnp.bfloat16)


def levels(stream_key, extent, cuts, smallest, largest):
    factor_of = 1.0
    for axis_at, parts in cuts:
        draws = jax.random.uniform(jax.random.fold_in(jax.random.fold_in(stream_key, 6), axis_at), (parts,), jnp.float32, smallest / len(cuts), largest / len(cuts))
        factor_of = factor_of * jnp.repeat(jnp.exp(draws), extent[axis_at] // parts).reshape((-1,) + (1,) * (len(extent) - 1 - axis_at))
    return factor_of


def scatter_about(rng, dims, scale, reach, pieces=(), held_as=jnp.bfloat16):
    factor_of = levels(rng, dims, pieces, -0.22, 0.18) if pieces else 1.0
    result = jax.random.normal(rng, dims, jnp.float32) * scale * factor_of
    return jnp.minimum(jnp.maximum(result, -reach), reach).astype(held_as)


def setup_inputs(seed: int = 0) -> dict:
    key_list = jax.random.split(jax.random.key(seed), 12)
    return {
        "source": draw_source(jax.random.fold_in(key_list[11], 71), 0),
        "diag_block": draw_diag_block(jax.random.fold_in(key_list[11], 71), 0),
        "link_time": scatter_about(key_list[2], (NT, NZ, NY, NX, DOF, DOF), (4 * DOF) ** -0.5, 0.25, ((0, 16), (1, 8), (2, 4))),
        "link_zaxis": scatter_about(key_list[3], (NT, NZ, NY, NX, DOF, DOF), (4 * DOF) ** -0.5, 0.25, ((0, 16), (1, 8), (2, 4))),
        "link_yaxis": scatter_about(key_list[4], (NT, NZ, NY, NX, DOF, DOF), (4 * DOF) ** -0.5, 0.25, ((0, 16), (1, 8), (2, 4))),
        "link_xaxis": scatter_about(key_list[5], (NT, NZ, NY, NX, DOF, DOF), (4 * DOF) ** -0.5, 0.25, ((0, 16), (1, 8), (2, 4))),
        "prolong": scatter_about(key_list[6], (NT, NZ, NY, NX, DOF, DC), (2 * DOF) ** -0.5, 0.375, ((0, 16), (1, 8), (2, 4))),
        "top_diag": scatter_about(key_list[7], (N_TA, N_GZ, N_YX, DC, DC), DC ** -0.5, 0.5, ((0, 16), (1, 8), (2, 4))),
        "top_time": scatter_about(key_list[8], (N_TA, N_GZ, N_YX, DC, DC), (4 * DC) ** -0.5, 0.25, ((0, 16), (1, 8), (2, 4))),
        "top_zaxis": scatter_about(key_list[9], (N_TA, N_GZ, N_YX, DC, DC), (4 * DC) ** -0.5, 0.25, ((0, 16), (1, 8), (2, 4))),
        "top_yaxis": scatter_about(key_list[10], (N_TA, N_GZ, N_YX, DC, DC), (4 * DC) ** -0.5, 0.25, ((0, 16), (1, 8), (2, 4))),
    }


def multiply(blocks, vector_in):
    return jnp.einsum("tzyxij,tzyxrj->tzyxri", blocks.astype(jnp.float32), vector_in.astype(jnp.float32), precision=lax.Precision.HIGHEST)


def transposed(blocks, vector_in):
    return jnp.einsum("tzyxji,tzyxrj->tzyxri", blocks.astype(jnp.float32), vector_in.astype(jnp.float32), precision=lax.Precision.HIGHEST)


def coarse_mult(blocks, vector_in):
    return jnp.einsum("azyij,azyrj->azyri", blocks.astype(jnp.float32), vector_in, precision=lax.Precision.HIGHEST)


def coarse_trans(blocks, vector_in):
    return jnp.einsum("azyji,azyrj->azyri", blocks.astype(jnp.float32), vector_in, precision=lax.Precision.HIGHEST)


def apply_dirac(vector_in, diag_block, link_list):
    summed = multiply(diag_block, vector_in)
    for dim_index, blocks in enumerate(link_list):
        summed = summed + multiply(blocks, jnp.roll(vector_in, -1, dim_index))
        backed = transposed(blocks, vector_in).astype(jnp.bfloat16)
        summed = summed + jnp.roll(backed, 1, dim_index).astype(jnp.float32)
    return summed


def reference(source, diag_block, link_time, link_zaxis, link_yaxis, link_xaxis, prolong, top_diag, top_time, top_zaxis, top_yaxis):
    link_list = (link_time, link_zaxis, link_yaxis, link_xaxis)
    grouped_src = source.reshape(N_TA, LT_DEV, NZ, NY, NX, RHS, DOF).astype(jnp.float32)
    grouped_pro = prolong.reshape(N_TA, LT_DEV, NZ, NY, NX, DOF, DC).astype(jnp.float32)
    restricted = jnp.einsum("alzyxij,alzyxri->azyrj", grouped_pro, grouped_src, precision=lax.Precision.HIGHEST)
    correction = coarse_mult(top_diag, restricted)
    for dim_index, blocks in enumerate((top_time, top_zaxis, top_yaxis)):
        correction = correction + coarse_mult(blocks, jnp.roll(restricted, -1, dim_index))
        correction = correction + jnp.roll(coarse_trans(blocks, restricted), 1, dim_index)
    coarse_fix = correction.astype(jnp.bfloat16)
    lifted = jnp.einsum("alzyxij,azyrj->alzyxri", grouped_pro, coarse_fix.astype(jnp.float32), precision=lax.Precision.HIGHEST)
    lifted = lifted.reshape(NT, NZ, NY, NX, RHS, DOF).astype(jnp.bfloat16)
    applied = apply_dirac(lifted, diag_block, link_list)
    resid = (source.astype(jnp.float32) - applied).astype(jnp.bfloat16)
    image = apply_dirac(resid, diag_block, link_list)
    resid_wide = resid.astype(jnp.float32)
    cross_term = jnp.sum(image * resid_wide, axis=(0, 1, 2, 3, 5))
    energy = jnp.sum(image * image, axis=(0, 1, 2, 3, 5))
    factor = cross_term / (energy + 1e-6)
    update = lifted.astype(jnp.float32) + factor[:, None] * resid_wide
    remainder = resid_wide - factor[:, None] * image
    return update, remainder
```

```python
import itertools

import jax
import jax.numpy as jnp
from jax import lax
from jax.experimental import pallas as pl
from jax.experimental.pallas import tpu as pltpu
from jax.sharding import PartitionSpec as P

MESH = pl.DeviceIdType.MESH
F32 = jnp.float32
BF16 = jnp.bfloat16

NX, RHS, DOF = 12, 32, 128
CHUNKS = 2
SPAN = NX // CHUNKS
SIZES = {"core": 2, "x": 4, "y": 8, "z": 8}
PHASES = (("core", "x"), ("y",), ("z",))


def offsets_of(phase):
    every = itertools.product(*(range(SIZES[axis]) for axis in phase))
    return [dict(zip(phase, step)) for step in every if any(step)]


COUNTS = [len(offsets_of(phase)) for phase in PHASES]


def forward(vector, block):
    return lax.dot_general(vector, block, (((1,), (1,)), ((), ())), preferred_element_type=F32)


def adjoint(vector, block):
    return lax.dot_general(vector, block, (((1,), (0,)), ((), ())), preferred_element_type=F32)


def halves(value):
    high = value.astype(BF16)
    low = (value - high.astype(F32)).astype(BF16)
    return jnp.concatenate([high, low], axis=0)


def fold(value):
    return value[:RHS] + value[RHS:]


def kernel(
    src_h, diag_h, lt_h, lz_h, ly_h, lx_h, pro_h, td_h, tt_h, tz_h, ty_h,
    lifted_o, resid_o, image_o, factor_o,
    src, diag, links, pro, tops,
    field, back, field_in, back_in, total, image, factor,
    coarse, coarse_in, hop_in,
    sum_out, sum_in,
    load_sem, store_sem,
    coarse_send, coarse_recv, field_send, field_recv, back_send, back_recv,
    sum_send, sum_recv,
):
    ta, gz, yx = lax.axis_index("ta"), lax.axis_index("gz"), lax.axis_index("yx")

    def at(ta_at, gz_at, yx_at):
        return (ta_at, gz_at, yx_at)

    plus = (
        at(lax.rem(ta + 1, 16), gz, yx),
        at(ta, lax.rem(gz + 1, 8), yx),
        at(ta, gz, lax.rem(yx + 1, 4)),
    )
    minus = (
        at(lax.rem(ta + 15, 16), gz, yx),
        at(ta, lax.rem(gz + 7, 8), yx),
        at(ta, gz, lax.rem(yx + 3, 4)),
    )
    here = {
        "core": lax.rem(gz, 2),
        "x": yx,
        "y": (ta // 8) * 4 + gz // 2,
        "z": lax.rem(ta, 8),
    }

    def partner(step):
        place = {
            axis: lax.rem(here[axis] + step.get(axis, 0), size) if step.get(axis, 0) else here[axis]
            for axis, size in SIZES.items()
        }
        return at(
            (place["y"] // 4) * 8 + place["z"],
            lax.rem(place["y"], 4) * 2 + place["core"],
            place["x"],
        )

    loads = {}
    pairs = (
        ("pro", pro_h, pro),
        ("src", src_h, src),
        ("tt", tt_h, tops.at[0]),
        ("tz", tz_h, tops.at[1]),
        ("ty", ty_h, tops.at[2]),
        ("td", td_h, tops.at[3]),
        ("lt", lt_h, links.at[0]),
        ("lz", lz_h, links.at[1]),
        ("ly", ly_h, links.at[2]),
        ("lx", lx_h, links.at[3]),
        ("diag", diag_h, diag),
    )
    for index, (name, source, target) in enumerate(pairs):
        loads[name] = pltpu.make_async_copy(source, target, load_sem.at[index])
        loads[name].start()

    barrier = pltpu.get_barrier_semaphore()
    greeted = list(plus) + list(minus)
    for phase in PHASES:
        greeted += [partner(step) for step in offsets_of(phase)]
    for device in greeted:
        pl.semaphore_signal(barrier, inc=1, device_id=device, device_id_type=MESH)

    def remote(source, target, send, recv, device):
        return pltpu.make_async_remote_copy(
            src_ref=source, dst_ref=target, send_sem=send, recv_sem=recv,
            device_id=device, device_id_type=MESH,
        )

    loads["pro"].wait()
    loads["src"].wait()
    restricted = adjoint(src[0], pro[0])
    for n in range(1, NX):
        restricted += adjoint(src[n], pro[n])
    coarse[0] = restricted
    split = halves(restricted)
    for mu, name in enumerate(("tt", "tz", "ty")):
        loads[name].wait()
        coarse[1 + mu] = fold(adjoint(split, tops[mu]))

    pl.semaphore_wait(barrier, len(greeted))

    coarse_copies = []
    for mu in range(3):
        coarse_copies.append(
            remote(coarse.at[0], coarse_in.at[mu], coarse_send.at[mu], coarse_recv.at[mu], minus[mu])
        )
        coarse_copies.append(
            remote(coarse.at[1 + mu], hop_in.at[mu], coarse_send.at[3 + mu], coarse_recv.at[3 + mu], plus[mu])
        )
    for copy in coarse_copies:
        copy.start()
    loads["td"].wait()
    correction = fold(forward(split, tops[3]))
    for mu in (2, 1, 0):
        coarse_copies[2 * mu].wait_recv()
        correction += fold(forward(halves(coarse_in[mu]), tops[mu]))
        coarse_copies[2 * mu + 1].wait_recv()
        correction += hop_in[mu]
    coarse_fix = correction.astype(BF16)

    def span(part):
        return pl.ds(part * SPAN, SPAN)

    def field_copy(turn, mu, part):
        return remote(
            field.at[turn, span(part)], field_in.at[turn, mu, span(part)],
            field_send.at[turn, mu, part], field_recv.at[turn, mu, part], minus[mu],
        )

    def back_copy(turn, mu, part):
        return remote(
            back.at[turn, mu, span(part)], back_in.at[turn, mu, span(part)],
            back_send.at[turn, mu, part], back_recv.at[turn, mu, part], plus[mu],
        )

    def sites(part):
        return range(part * SPAN, (part + 1) * SPAN)

    def send_field(turn, part):
        for mu in range(3):
            field_copy(turn, mu, part).start()

    def send_back(turn, mu, part):
        for n in sites(part):
            back[turn, mu, n] = adjoint(field[turn, n], links[mu, n]).astype(BF16)
        back_copy(turn, mu, part).start()

    def local_terms(turn):
        for n in range(NX):
            after, before = (n + 1) % NX, (n - 1) % NX
            value = forward(field[turn, n], diag[n])
            value += forward(field[turn, after], links[3, n])
            value += adjoint(field[turn, before], links[3, before]).astype(BF16).astype(F32)
            total[n] = value

    def arrived(turn, mu, part):
        field_copy(turn, mu, part).wait_recv()
        back_copy(turn, mu, part).wait_recv()

    def hop_terms(turn, mu, n):
        return forward(field_in[turn, mu, n], links[mu, n]) + back_in[turn, mu, n].astype(F32)

    def near_terms(turn):
        for mu in (2, 1):
            for part in range(CHUNKS):
                arrived(turn, mu, part)
                for n in sites(part):
                    total[n] += hop_terms(turn, mu, n)

    for part in range(CHUNKS):
        for n in sites(part):
            field[0, n] = forward(coarse_fix, pro[n]).astype(BF16)
        send_field(0, part)
    for mu, name in enumerate(("lt", "lz", "ly")):
        loads[name].wait()
        for part in range(CHUNKS):
            send_back(0, mu, part)
    store_lifted = pltpu.make_async_copy(field.at[0], lifted_o, store_sem.at[0])
    store_lifted.start()
    loads["lx"].wait()
    loads["diag"].wait()
    local_terms(0)
    near_terms(0)
    for part in range(CHUNKS):
        arrived(0, 0, part)
        for n in sites(part):
            applied = total[n] + hop_terms(0, 0, n)
            field[1, n] = (src[n].astype(F32) - applied).astype(BF16)
        send_field(1, part)
        send_back(1, 0, part)
    for mu in (1, 2):
        for part in range(CHUNKS):
            send_back(1, mu, part)
    store_resid = pltpu.make_async_copy(field.at[1], resid_o, store_sem.at[1])
    store_resid.start()

    local_terms(1)
    near_terms(1)
    cross = jnp.zeros((RHS, DOF), F32)
    energy = jnp.zeros((RHS, DOF), F32)
    for part in range(CHUNKS):
        arrived(1, 0, part)
        for n in sites(part):
            value = total[n] + hop_terms(1, 0, n)
            image[n] = value
            cross += value * field[1, n].astype(F32)
            energy += value * value
    store_image = pltpu.make_async_copy(image, image_o, store_sem.at[2])
    store_image.start()

    row = lax.broadcasted_iota(jnp.int32, (RHS, DOF), 0)
    lane = lax.broadcasted_iota(jnp.int32, (RHS, DOF), 1)
    cross_at = jnp.sum(cross, axis=1, keepdims=True)
    energy_at = jnp.sum(energy, axis=1, keepdims=True)
    laid = jnp.where(lane == row, cross_at, jnp.where(lane == row + RHS, energy_at, 0.0))
    sums = jnp.sum(laid, axis=0, keepdims=True)

    base = 0
    for index, phase in enumerate(PHASES):
        sum_out[index] = sums
        copies = []
        for slot, step in enumerate(offsets_of(phase)):
            copies.append(
                remote(
                    sum_out.at[index], sum_in.at[base + slot],
                    sum_send.at[base + slot], sum_recv.at[base + slot], partner(step),
                )
            )
        for copy in copies:
            copy.start()
        for copy in copies:
            copy.wait_recv()
        for slot in range(len(copies)):
            sums = sums + sum_in[base + slot]
        for copy in copies:
            copy.wait_send()
        base += len(copies)

    wide = jnp.broadcast_to(sums, (RHS, DOF))
    cross_sum = jnp.sum(jnp.where(lane == row, wide, 0.0), axis=1, keepdims=True)
    energy_sum = jnp.sum(jnp.where(lane == row + RHS, wide, 0.0), axis=1, keepdims=True)
    factor[...] = jnp.broadcast_to(cross_sum / (energy_sum + 1e-06), (RHS, DOF))
    store_factor = pltpu.make_async_copy(factor, factor_o, store_sem.at[3])
    store_factor.start()

    for copy in coarse_copies:
        copy.wait_send()
    for turn in range(2):
        for mu in range(3):
            for part in range(CHUNKS):
                field_copy(turn, mu, part).wait_send()
                back_copy(turn, mu, part).wait_send()
    for copy in (store_lifted, store_resid, store_image, store_factor):
        copy.wait()


def body(source, diag_block, link_time, link_zaxis, link_yaxis, link_xaxis, prolong,
         top_diag, top_time, top_zaxis, top_yaxis):
    shape = source.shape
    blocks = [
        value.reshape(NX, DOF, DOF)
        for value in (diag_block, link_time, link_zaxis, link_yaxis, link_xaxis, prolong)
    ]
    tops = [value.reshape(DOF, DOF) for value in (top_diag, top_time, top_zaxis, top_yaxis)]
    vmem, dma = pltpu.VMEM, pltpu.SemaphoreType.DMA
    total = sum(COUNTS)
    lifted, resid, image, factor = pl.pallas_call(
        kernel,
        out_shape=(
            jax.ShapeDtypeStruct((NX, RHS, DOF), BF16),
            jax.ShapeDtypeStruct((NX, RHS, DOF), BF16),
            jax.ShapeDtypeStruct((NX, RHS, DOF), F32),
            jax.ShapeDtypeStruct((RHS, DOF), F32),
        ),
        in_specs=[pl.BlockSpec(memory_space=pl.ANY)] * 11,
        out_specs=[pl.BlockSpec(memory_space=pl.ANY)] * 4,
        scratch_shapes=[
            vmem((NX, RHS, DOF), BF16),
            vmem((NX, DOF, DOF), BF16),
            vmem((4, NX, DOF, DOF), BF16),
            vmem((NX, DOF, DOF), BF16),
            vmem((4, DOF, DOF), BF16),
            vmem((2, NX, RHS, DOF), BF16),
            vmem((2, 3, NX, RHS, DOF), BF16),
            vmem((2, 3, NX, RHS, DOF), BF16),
            vmem((2, 3, NX, RHS, DOF), BF16),
            vmem((NX, RHS, DOF), F32),
            vmem((NX, RHS, DOF), F32),
            vmem((RHS, DOF), F32),
            vmem((4, RHS, DOF), F32),
            vmem((3, RHS, DOF), F32),
            vmem((3, RHS, DOF), F32),
            vmem((len(PHASES), 1, DOF), F32),
            vmem((total, 1, DOF), F32),
            dma((11,)),
            dma((4,)),
            dma((6,)),
            dma((6,)),
            dma((2, 3, CHUNKS)),
            dma((2, 3, CHUNKS)),
            dma((2, 3, CHUNKS)),
            dma((2, 3, CHUNKS)),
            dma((total,)),
            dma((total,)),
        ],
        compiler_params=pltpu.CompilerParams(
            collective_id=0, has_side_effects=True, vmem_limit_bytes=32 * 1024 * 1024
        ),
        name="smooth",
    )(source.reshape(NX, RHS, DOF), *blocks, *tops)
    wide = resid.astype(F32)
    update = lifted.astype(F32) + factor * wide
    remainder = wide - factor * image
    return update.reshape(shape), remainder.reshape(shape)


def solution(mesh):
    field = P("ta", "gz", "yx", None, None, None)
    top = P("ta", "gz", "yx", None, None)
    return jax.shard_map(
        body, mesh=mesh, in_specs=(field,) * 7 + (top,) * 4, out_specs=(field, field), check_vma=False
    )
```

```python
import itertools

import jax
import jax.numpy as jnp
from jax import lax
from jax.experimental import pallas as pl
from jax.experimental.pallas import tpu as pltpu
from jax.sharding import PartitionSpec as P

MESH = pl.DeviceIdType.MESH
F32 = jnp.float32
BF16 = jnp.bfloat16

NX, RHS, DOF = 12, 32, 128
CHUNKS = 2
SPAN = NX // CHUNKS
SIZES = {"core": 2, "x": 4, "y": 8, "z": 8}
PHASES = (("core", "x"), ("y",), ("z",))


def offsets_of(phase):
    every = itertools.product(*(range(SIZES[axis]) for axis in phase))
    return [dict(zip(phase, step)) for step in every if any(step)]


COUNTS = [len(offsets_of(phase)) for phase in PHASES]


def forward(vector, block):
    return lax.dot_general(vector, block, (((1,), (1,)), ((), ())), preferred_element_type=F32)


def adjoint(vector, block):
    return lax.dot_general(vector, block, (((1,), (0,)), ((), ())), preferred_element_type=F32)


def halves(value):
    high = value.astype(BF16)
    low = (value - high.astype(F32)).astype(BF16)
    return jnp.concatenate([high, low], axis=0)


def fold(value):
    return value[:RHS] + value[RHS:]


def kernel(
    src_h, diag_h, lt_h, lz_h, ly_h, lx_h, pro_h, td_h, tt_h, tz_h, ty_h,
    lifted_o, resid_o, image_o, factor_o,
    src, diag, links, pro, tops,
    field, back, field_in, back_in, total, image, factor,
    coarse, coarse_in, hop_in,
    sum_out, sum_in,
    load_sem, store_sem,
    coarse_send, coarse_recv, field_send, field_recv, back_send, back_recv,
    sum_send, sum_recv,
):
    ta, gz, yx = lax.axis_index("ta"), lax.axis_index("gz"), lax.axis_index("yx")

    def at(ta_at, gz_at, yx_at):
        return (ta_at, gz_at, yx_at)

    plus = (
        at(lax.rem(ta + 1, 16), gz, yx),
        at(ta, lax.rem(gz + 1, 8), yx),
        at(ta, gz, lax.rem(yx + 1, 4)),
    )
    minus = (
        at(lax.rem(ta + 15, 16), gz, yx),
        at(ta, lax.rem(gz + 7, 8), yx),
        at(ta, gz, lax.rem(yx + 3, 4)),
    )
    here = {
        "core": lax.rem(gz, 2),
        "x": yx,
        "y": (ta // 8) * 4 + gz // 2,
        "z": lax.rem(ta, 8),
    }

    def partner(step):
        place = {
            axis: lax.rem(here[axis] + step.get(axis, 0), size) if step.get(axis, 0) else here[axis]
            for axis, size in SIZES.items()
        }
        return at(
            (place["y"] // 4) * 8 + place["z"],
            lax.rem(place["y"], 4) * 2 + place["core"],
            place["x"],
        )

    loads = {}
    pairs = (
        ("pro", pro_h, pro),
        ("src", src_h, src),
        ("tt", tt_h, tops.at[0]),
        ("tz", tz_h, tops.at[1]),
        ("ty", ty_h, tops.at[2]),
        ("td", td_h, tops.at[3]),
        ("lt", lt_h, links.at[0]),
        ("lz", lz_h, links.at[1]),
        ("ly", ly_h, links.at[2]),
        ("lx", lx_h, links.at[3]),
        ("diag", diag_h, diag),
    )
    for index, (name, source, target) in enumerate(pairs):
        loads[name] = pltpu.make_async_copy(source, target, load_sem.at[index])
        loads[name].start()

    barrier = pltpu.get_barrier_semaphore()
    greeted = list(plus) + list(minus)
    for phase in PHASES:
        greeted += [partner(step) for step in offsets_of(phase)]
    for device in greeted:
        pl.semaphore_signal(barrier, inc=1, device_id=device, device_id_type=MESH)

    def remote(source, target, send, recv, device):
        return pltpu.make_async_remote_copy(
            src_ref=source, dst_ref=target, send_sem=send, recv_sem=recv,
            device_id=device, device_id_type=MESH,
        )

    loads["pro"].wait()
    loads["src"].wait()
    restricted = adjoint(src[0], pro[0])
    for n in range(1, NX):
        restricted += adjoint(src[n], pro[n])
    coarse[0] = restricted
    split = halves(restricted)
    for mu, name in enumerate(("tt", "tz", "ty")):
        loads[name].wait()
        coarse[1 + mu] = fold(adjoint(split, tops[mu]))

    pl.semaphore_wait(barrier, len(greeted))

    coarse_copies = []
    for mu in range(3):
        coarse_copies.append(
            remote(coarse.at[0], coarse_in.at[mu], coarse_send.at[mu], coarse_recv.at[mu], minus[mu])
        )
        coarse_copies.append(
            remote(coarse.at[1 + mu], hop_in.at[mu], coarse_send.at[3 + mu], coarse_recv.at[3 + mu], plus[mu])
        )
    for copy in coarse_copies:
        copy.start()
    loads["td"].wait()
    correction = fold(forward(split, tops[3]))
    for mu in (2, 1, 0):
        coarse_copies[2 * mu].wait_recv()
        correction += fold(forward(halves(coarse_in[mu]), tops[mu]))
        coarse_copies[2 * mu + 1].wait_recv()
        correction += hop_in[mu]
    coarse_fix = correction.astype(BF16)

    def span(part):
        return pl.ds(part * SPAN, SPAN)

    def field_copy(turn, mu, part):
        return remote(
            field.at[turn, span(part)], field_in.at[turn, mu, span(part)],
            field_send.at[turn, mu, part], field_recv.at[turn, mu, part], minus[mu],
        )

    def back_copy(turn, mu, part):
        return remote(
            back.at[turn, mu, span(part)], back_in.at[turn, mu, span(part)],
            back_send.at[turn, mu, part], back_recv.at[turn, mu, part], plus[mu],
        )

    def sites(part):
        return range(part * SPAN, (part + 1) * SPAN)

    def send_field(turn, part):
        for mu in range(3):
            field_copy(turn, mu, part).start()

    def send_back(turn, mu, part):
        for n in sites(part):
            back[turn, mu, n] = adjoint(field[turn, n], links[mu, n]).astype(BF16)
        back_copy(turn, mu, part).start()

    def local_terms(turn):
        for n in range(NX):
            after, before = (n + 1) % NX, (n - 1) % NX
            value = forward(field[turn, n], diag[n])
            value += forward(field[turn, after], links[3, n])
            value += adjoint(field[turn, before], links[3, before]).astype(BF16).astype(F32)
            total[n] = value

    def arrived(turn, mu, part):
        field_copy(turn, mu, part).wait_recv()
        back_copy(turn, mu, part).wait_recv()

    def hop_terms(turn, mu, n):
        return forward(field_in[turn, mu, n], links[mu, n]) + back_in[turn, mu, n].astype(F32)

    def near_terms(turn):
        for mu in (2, 1):
            for part in range(CHUNKS):
                arrived(turn, mu, part)
                for n in sites(part):
                    total[n] += hop_terms(turn, mu, n)

    for part in range(CHUNKS):
        for n in sites(part):
            field[0, n] = forward(coarse_fix, pro[n]).astype(BF16)
        send_field(0, part)
    for mu, name in enumerate(("lt", "lz", "ly")):
        loads[name].wait()
        for part in range(CHUNKS):
            send_back(0, mu, part)
    store_lifted = pltpu.make_async_copy(field.at[0], lifted_o, store_sem.at[0])
    store_lifted.start()
    loads["lx"].wait()
    loads["diag"].wait()
    local_terms(0)
    near_terms(0)
    for part in range(CHUNKS):
        arrived(0, 0, part)
        for n in sites(part):
            applied = total[n] + hop_terms(0, 0, n)
            field[1, n] = (src[n].astype(F32) - applied).astype(BF16)
        send_field(1, part)
        send_back(1, 0, part)
    for mu in (1, 2):
        for part in range(CHUNKS):
            send_back(1, mu, part)
    store_resid = pltpu.make_async_copy(field.at[1], resid_o, store_sem.at[1])
    store_resid.start()

    local_terms(1)
    near_terms(1)
    cross = jnp.zeros((RHS, DOF), F32)
    energy = jnp.zeros((RHS, DOF), F32)
    for part in range(CHUNKS):
        arrived(1, 0, part)
        for n in sites(part):
            value = total[n] + hop_terms(1, 0, n)
            image[n] = value
            cross += value * field[1, n].astype(F32)
            energy += value * value
    store_image = pltpu.make_async_copy(image, image_o, store_sem.at[2])
    store_image.start()

    row = lax.broadcasted_iota(jnp.int32, (RHS, DOF), 0)
    lane = lax.broadcasted_iota(jnp.int32, (RHS, DOF), 1)
    cross_at = jnp.sum(cross, axis=1, keepdims=True)
    energy_at = jnp.sum(energy, axis=1, keepdims=True)
    laid = jnp.where(lane == row, cross_at, jnp.where(lane == row + RHS, energy_at, 0.0))
    sums = jnp.sum(laid, axis=0, keepdims=True)

    base = 0
    sum_copies = []
    for index, phase in enumerate(PHASES):
        sum_out[index] = sums
        copies = []
        for slot, step in enumerate(offsets_of(phase)):
            copies.append(
                remote(
                    sum_out.at[index], sum_in.at[base + slot],
                    sum_send.at[base + slot], sum_recv.at[base + slot], partner(step),
                )
            )
        for copy in copies:
            copy.start()
        for copy in copies:
            copy.wait_recv()
        for slot in range(len(copies)):
            sums = sums + sum_in[base + slot]
        sum_copies += copies
        base += len(copies)

    wide = jnp.broadcast_to(sums, (RHS, DOF))
    cross_sum = jnp.sum(jnp.where(lane == row, wide, 0.0), axis=1, keepdims=True)
    energy_sum = jnp.sum(jnp.where(lane == row + RHS, wide, 0.0), axis=1, keepdims=True)
    factor[...] = jnp.broadcast_to(cross_sum / (energy_sum + 1e-06), (RHS, DOF))
    store_factor = pltpu.make_async_copy(factor, factor_o, store_sem.at[3])
    store_factor.start()

    for copy in coarse_copies + sum_copies:
        copy.wait_send()
    for turn in range(2):
        for mu in range(3):
            for part in range(CHUNKS):
                field_copy(turn, mu, part).wait_send()
                back_copy(turn, mu, part).wait_send()
    for copy in (store_lifted, store_resid, store_image, store_factor):
        copy.wait()


def body(source, diag_block, link_time, link_zaxis, link_yaxis, link_xaxis, prolong,
         top_diag, top_time, top_zaxis, top_yaxis):
    shape = source.shape
    blocks = [
        value.reshape(NX, DOF, DOF)
        for value in (diag_block, link_time, link_zaxis, link_yaxis, link_xaxis, prolong)
    ]
    tops = [value.reshape(DOF, DOF) for value in (top_diag, top_time, top_zaxis, top_yaxis)]
    vmem, dma = pltpu.VMEM, pltpu.SemaphoreType.DMA
    total = sum(COUNTS)
    lifted, resid, image, factor = pl.pallas_call(
        kernel,
        out_shape=(
            jax.ShapeDtypeStruct((NX, RHS, DOF), BF16),
            jax.ShapeDtypeStruct((NX, RHS, DOF), BF16),
            jax.ShapeDtypeStruct((NX, RHS, DOF), F32),
            jax.ShapeDtypeStruct((RHS, DOF), F32),
        ),
        in_specs=[pl.BlockSpec(memory_space=pltpu.HBM)] * 11,
        out_specs=[pl.BlockSpec(memory_space=pl.ANY)] * 4,
        scratch_shapes=[
            vmem((NX, RHS, DOF), BF16),
            vmem((NX, DOF, DOF), BF16),
            vmem((4, NX, DOF, DOF), BF16),
            vmem((NX, DOF, DOF), BF16),
            vmem((4, DOF, DOF), BF16),
            vmem((2, NX, RHS, DOF), BF16),
            vmem((2, 3, NX, RHS, DOF), BF16),
            vmem((2, 3, NX, RHS, DOF), BF16),
            vmem((2, 3, NX, RHS, DOF), BF16),
            vmem((NX, RHS, DOF), F32),
            vmem((NX, RHS, DOF), F32),
            vmem((RHS, DOF), F32),
            vmem((4, RHS, DOF), F32),
            vmem((3, RHS, DOF), F32),
            vmem((3, RHS, DOF), F32),
            vmem((len(PHASES), 1, DOF), F32),
            vmem((total, 1, DOF), F32),
            dma((11,)),
            dma((4,)),
            dma((6,)),
            dma((6,)),
            dma((2, 3, CHUNKS)),
            dma((2, 3, CHUNKS)),
            dma((2, 3, CHUNKS)),
            dma((2, 3, CHUNKS)),
            dma((total,)),
            dma((total,)),
        ],
        compiler_params=pltpu.CompilerParams(
            collective_id=0, has_side_effects=True, vmem_limit_bytes=60 * 1024 * 1024
        ),
        name="smooth",
    )(source.reshape(NX, RHS, DOF), *blocks, *tops)
    wide = resid.astype(F32)
    update = lifted.astype(F32) + factor * wide
    remainder = wide - factor * image
    return update.reshape(shape), remainder.reshape(shape)


def solution(mesh):
    field = P("ta", "gz", "yx", None, None, None)
    top = P("ta", "gz", "yx", None, None)
    return jax.shard_map(
        body, mesh=mesh, in_specs=(field,) * 7 + (top,) * 4, out_specs=(field, field), check_vma=False
    )
```

```python
import itertools

import jax
import jax.numpy as jnp
from jax import lax
from jax.experimental import pallas as pl
from jax.experimental.pallas import tpu as pltpu
from jax.sharding import PartitionSpec as P

MESH = pl.DeviceIdType.MESH
F32 = jnp.float32
BF16 = jnp.bfloat16

NX, RHS, DOF = 12, 32, 128
CHUNKS = 2
LOADS = 4
SPAN = NX // CHUNKS
SIZES = {"core": 2, "x": 4, "y": 8, "z": 8}
PHASES = (("z",), ("core", "x", "y"))


def offsets_of(phase):
    every = itertools.product(*(range(SIZES[axis]) for axis in phase))
    return [dict(zip(phase, step)) for step in every if any(step)]


COUNTS = [len(offsets_of(phase)) for phase in PHASES]


def forward(vector, block):
    return lax.dot_general(vector, block, (((1,), (1,)), ((), ())), preferred_element_type=F32)


def adjoint(vector, block):
    return lax.dot_general(vector, block, (((1,), (0,)), ((), ())), preferred_element_type=F32)


def halves(value):
    high = value.astype(BF16)
    low = (value - high.astype(F32)).astype(BF16)
    return jnp.concatenate([high, low], axis=0)


def fold(value):
    return value[:RHS] + value[RHS:]


def kernel(
    src_h, diag_h, lt_h, lz_h, ly_h, lx_h, pro_h, td_h, tt_h, tz_h, ty_h,
    lifted_o, resid_o, image_o, factor_o,
    src, diag, links, pro, tops,
    field, back, field_in, back_in, total, image, factor,
    coarse, coarse_in, hop_in,
    sum_out, sum_in,
    load_sem, store_sem,
    coarse_send, coarse_recv, field_send, field_recv, back_send, back_recv,
    sum_send, sum_recv,
    relay_in, relay_send, relay_recv, late_in, met,
):
    ta, gz, yx = lax.axis_index("ta"), lax.axis_index("gz"), lax.axis_index("yx")

    def at(ta_at, gz_at, yx_at):
        return (ta_at, gz_at, yx_at)

    plus = (
        at(lax.rem(ta + 1, 16), gz, yx),
        at(ta, lax.rem(gz + 1, 8), yx),
        at(ta, gz, lax.rem(yx + 1, 4)),
    )
    minus = (
        at(lax.rem(ta + 15, 16), gz, yx),
        at(ta, lax.rem(gz + 7, 8), yx),
        at(ta, gz, lax.rem(yx + 3, 4)),
    )
    here = {
        "core": lax.rem(gz, 2),
        "x": yx,
        "y": (ta // 8) * 4 + gz // 2,
        "z": lax.rem(ta, 8),
    }

    def partner(step):
        place = {
            axis: lax.rem(here[axis] + step.get(axis, 0), size) if step.get(axis, 0) else here[axis]
            for axis, size in SIZES.items()
        }
        return at(
            (place["y"] // 4) * 8 + place["z"],
            lax.rem(place["y"], 4) * 2 + place["core"],
            place["x"],
        )

    y, z = here["y"], here["z"]
    low, high = z == 0, z == 7
    across = partner({"y": 4})
    below, above = partner({"z": 7}), partner({"z": 1})

    pieces = []
    loads = {}

    def load(name, source, target):
        copy = pltpu.make_async_copy(source, target, load_sem.at[len(pieces)])
        copy.start()
        pieces.append(name)
        loads.setdefault(name, []).append(copy)

    def loaded(name):
        for copy in loads[name]:
            copy.wait()

    for part in range(LOADS):
        some = pl.ds(part * (NX // LOADS), NX // LOADS)
        load(("pro", part), pro_h.at[some], pro.at[some])
        load(("src", part), src_h.at[some], src.at[some])
    load("tt", tt_h, tops.at[0])
    load("tz", tz_h, tops.at[1])
    load("ty", ty_h, tops.at[2])
    load("td", td_h, tops.at[3])
    load("lt", lt_h, links.at[0])
    load("lz", lz_h, links.at[1])
    load("ly", ly_h, links.at[2])
    load("lx", lx_h, links.at[3])
    load("diag", diag_h, diag)

    def signal(semaphore, device):
        pl.semaphore_signal(semaphore, inc=1, device_id=device, device_id_type=MESH)

    barrier = pltpu.get_barrier_semaphore()
    for device in [plus[1], minus[1], plus[2], minus[2], partner({"y": 1}), partner({"y": 7})]:
        signal(barrier, device)
    for step in offsets_of(("core", "x")):
        signal(barrier, partner(step))

    @pl.when(low)
    def _():
        signal(barrier, minus[0])
        signal(barrier, below)
        signal(barrier, across)

    @pl.when(jnp.logical_not(low))
    def _():
        signal(barrier, minus[0])

    @pl.when(jnp.logical_not(high))
    def _():
        signal(barrier, plus[0])

    greetings = 13 + jnp.where(high, 3, 2)

    def remote(source, target, send, recv, device):
        return pltpu.make_async_remote_copy(
            src_ref=source, dst_ref=target, send_sem=send, recv_sem=recv,
            device_id=device, device_id_type=MESH,
        )

    restricted = jnp.zeros((RHS, DOF), F32)
    for part in range(LOADS):
        loaded(("pro", part))
        loaded(("src", part))
        for n in range(part * (NX // LOADS), (part + 1) * (NX // LOADS)):
            restricted += adjoint(src[n], pro[n])
    coarse[0] = restricted
    split = halves(restricted)
    for mu, name in enumerate(("tt", "tz", "ty")):
        loaded(name)
        coarse[1 + mu] = fold(adjoint(split, tops[mu]))

    pl.semaphore_wait(barrier, greetings)

    @pl.when(high)
    def _():
        signal(late_in, above)

    signal(met.at[0], partner({"y": 1}))
    signal(met.at[0], partner({"y": 7}))

    @pl.when(jnp.logical_not(low))
    def _():
        signal(met.at[0], below)

    @pl.when(jnp.logical_not(jnp.logical_or(low, high)))
    def _():
        signal(met.at[0], above)

    def value_copy(mu, device):
        return remote(coarse.at[0], coarse_in.at[mu], coarse_send.at[mu], coarse_recv.at[mu], device)

    def hop_copy(mu):
        return remote(
            coarse.at[1 + mu], hop_in.at[mu], coarse_send.at[3 + mu], coarse_recv.at[3 + mu], plus[mu]
        )

    hop_copy(0).start()
    to_relay = remote(coarse.at[0], relay_in, relay_send.at[0], relay_recv, across)
    from_relay = remote(relay_in, coarse_in.at[0], relay_send.at[1], coarse_recv.at[0], below)

    @pl.when(low)
    def _():
        to_relay.start()

    @pl.when(jnp.logical_not(low))
    def _():
        value_copy(0, minus[0]).start()

    for mu in (1, 2):
        value_copy(mu, minus[mu]).start()
        hop_copy(mu).start()

    @pl.when(low)
    def _():
        to_relay.wait_recv()
        pl.semaphore_wait(late_in, 1)
        from_relay.start()
        signal(met.at[0], above)

    loaded("td")
    correction = fold(forward(split, tops[3]))
    for mu in (2, 1, 0):
        value_copy(mu, minus[mu]).wait_recv()
        correction += fold(forward(halves(coarse_in[mu]), tops[mu]))
        hop_copy(mu).wait_recv()
        correction += hop_in[mu]
    coarse_fix = correction.astype(BF16)

    def span(part):
        return pl.ds(part * SPAN, SPAN)

    def field_copy(turn, mu, part):
        return remote(
            field.at[turn, span(part)], field_in.at[turn, mu, span(part)],
            field_send.at[turn, mu, part], field_recv.at[turn, mu, part], minus[mu],
        )

    def back_copy(turn, mu, part):
        return remote(
            back.at[turn, mu, span(part)], back_in.at[turn, mu, span(part)],
            back_send.at[turn, mu, part], back_recv.at[turn, mu, part], plus[mu],
        )

    def sites(part):
        return range(part * SPAN, (part + 1) * SPAN)

    def send_field(turn, part):
        for mu in range(3):
            field_copy(turn, mu, part).start()

    def send_back(turn, mu, part):
        for n in sites(part):
            back[turn, mu, n] = adjoint(field[turn, n], links[mu, n]).astype(BF16)
        back_copy(turn, mu, part).start()

    def local_terms(turn):
        for n in range(NX):
            after, before = (n + 1) % NX, (n - 1) % NX
            value = forward(field[turn, n], diag[n])
            value += forward(field[turn, after], links[3, n])
            value += adjoint(field[turn, before], links[3, before]).astype(BF16).astype(F32)
            total[n] = value

    def arrived(turn, mu, part):
        field_copy(turn, mu, part).wait_recv()
        back_copy(turn, mu, part).wait_recv()

    def hop_terms(turn, mu, n):
        return forward(field_in[turn, mu, n], links[mu, n]) + back_in[turn, mu, n].astype(F32)

    def near_terms(turn):
        for mu in (2, 1):
            for part in range(CHUNKS):
                arrived(turn, mu, part)
                for n in sites(part):
                    total[n] += hop_terms(turn, mu, n)

    for part in range(CHUNKS):
        for n in sites(part):
            field[0, n] = forward(coarse_fix, pro[n]).astype(BF16)
        send_field(0, part)
    for mu, name in enumerate(("lt", "lz", "ly")):
        loaded(name)
        for part in range(CHUNKS):
            send_back(0, mu, part)
    pl.semaphore_wait(met.at[0], 2 + jnp.where(jnp.logical_or(low, high), 1, 2))
    for step in ({"y": 2}, {"y": 6}, {"z": 2}, {"z": 6}):
        signal(met.at[1], partner(step))
    store_lifted = pltpu.make_async_copy(field.at[0], lifted_o, store_sem.at[0])
    store_lifted.start()
    loaded("lx")
    loaded("diag")
    local_terms(0)
    near_terms(0)
    for part in range(CHUNKS):
        arrived(0, 0, part)
        for n in sites(part):
            applied = total[n] + hop_terms(0, 0, n)
            field[1, n] = (src[n].astype(F32) - applied).astype(BF16)
        send_field(1, part)
        send_back(1, 0, part)
    for mu in (1, 2):
        for part in range(CHUNKS):
            send_back(1, mu, part)
    store_resid = pltpu.make_async_copy(field.at[1], resid_o, store_sem.at[1])
    store_resid.start()

    pl.semaphore_wait(met.at[1], 4)
    signal(met.at[2], across)

    local_terms(1)
    near_terms(1)
    cross = jnp.zeros((RHS, DOF), F32)
    energy = jnp.zeros((RHS, DOF), F32)
    for part in range(CHUNKS):
        arrived(1, 0, part)
        for n in sites(part):
            value = total[n] + hop_terms(1, 0, n)
            image[n] = value
            cross += value * field[1, n].astype(F32)
            energy += value * value
    store_image = pltpu.make_async_copy(image, image_o, store_sem.at[2])
    store_image.start()

    row = lax.broadcasted_iota(jnp.int32, (RHS, DOF), 0)
    lane = lax.broadcasted_iota(jnp.int32, (RHS, DOF), 1)
    cross_at = jnp.sum(cross, axis=1, keepdims=True)
    energy_at = jnp.sum(energy, axis=1, keepdims=True)
    laid = jnp.where(lane == row, cross_at, jnp.where(lane == row + RHS, energy_at, 0.0))
    sums = jnp.sum(laid, axis=0, keepdims=True)

    pl.semaphore_wait(met.at[2], 1)
    base = 0
    sum_copies = []
    for index, phase in enumerate(PHASES):
        sum_out[index] = sums
        copies = []
        for slot, step in enumerate(offsets_of(phase)):
            copies.append(
                remote(
                    sum_out.at[index], sum_in.at[base + slot],
                    sum_send.at[base + slot], sum_recv.at[base + slot], partner(step),
                )
            )
        for copy in copies:
            copy.start()
        for copy in copies:
            copy.wait_recv()
        for slot in range(len(copies)):
            sums = sums + sum_in[base + slot]
        sum_copies += copies
        base += len(copies)

    wide = jnp.broadcast_to(sums, (RHS, DOF))
    cross_sum = jnp.sum(jnp.where(lane == row, wide, 0.0), axis=1, keepdims=True)
    energy_sum = jnp.sum(jnp.where(lane == row + RHS, wide, 0.0), axis=1, keepdims=True)
    factor[...] = jnp.broadcast_to(cross_sum / (energy_sum + 1e-06), (RHS, DOF))
    store_factor = pltpu.make_async_copy(factor, factor_o, store_sem.at[3])
    store_factor.start()

    @pl.when(low)
    def _():
        to_relay.wait_send()
        from_relay.wait_send()

    @pl.when(jnp.logical_not(low))
    def _():
        value_copy(0, minus[0]).wait_send()

    for mu in range(3):
        if mu:
            value_copy(mu, minus[mu]).wait_send()
        hop_copy(mu).wait_send()
    for copy in sum_copies:
        copy.wait_send()
    for turn in range(2):
        for mu in range(3):
            for part in range(CHUNKS):
                field_copy(turn, mu, part).wait_send()
                back_copy(turn, mu, part).wait_send()
    for copy in (store_lifted, store_resid, store_image, store_factor):
        copy.wait()


def body(source, diag_block, link_time, link_zaxis, link_yaxis, link_xaxis, prolong,
         top_diag, top_time, top_zaxis, top_yaxis):
    shape = source.shape
    blocks = [
        value.reshape(NX, DOF, DOF)
        for value in (diag_block, link_time, link_zaxis, link_yaxis, link_xaxis, prolong)
    ]
    tops = [value.reshape(DOF, DOF) for value in (top_diag, top_time, top_zaxis, top_yaxis)]
    vmem, dma = pltpu.VMEM, pltpu.SemaphoreType.DMA
    total = sum(COUNTS)
    lifted, resid, image, factor = pl.pallas_call(
        kernel,
        out_shape=(
            jax.ShapeDtypeStruct((NX, RHS, DOF), BF16),
            jax.ShapeDtypeStruct((NX, RHS, DOF), BF16),
            jax.ShapeDtypeStruct((NX, RHS, DOF), F32),
            jax.ShapeDtypeStruct((RHS, DOF), F32),
        ),
        in_specs=[pl.BlockSpec(memory_space=pltpu.HBM)] * 11,
        out_specs=[pl.BlockSpec(memory_space=pl.ANY)] * 4,
        scratch_shapes=[
            vmem((NX, RHS, DOF), BF16),
            vmem((NX, DOF, DOF), BF16),
            vmem((4, NX, DOF, DOF), BF16),
            vmem((NX, DOF, DOF), BF16),
            vmem((4, DOF, DOF), BF16),
            vmem((2, NX, RHS, DOF), BF16),
            vmem((2, 3, NX, RHS, DOF), BF16),
            vmem((2, 3, NX, RHS, DOF), BF16),
            vmem((2, 3, NX, RHS, DOF), BF16),
            vmem((NX, RHS, DOF), F32),
            vmem((NX, RHS, DOF), F32),
            vmem((RHS, DOF), F32),
            vmem((4, RHS, DOF), F32),
            vmem((3, RHS, DOF), F32),
            vmem((3, RHS, DOF), F32),
            vmem((len(PHASES), 1, DOF), F32),
            vmem((total, 1, DOF), F32),
            dma((2 * LOADS + 9,)),
            dma((4,)),
            dma((6,)),
            dma((6,)),
            dma((2, 3, CHUNKS)),
            dma((2, 3, CHUNKS)),
            dma((2, 3, CHUNKS)),
            dma((2, 3, CHUNKS)),
            dma((total,)),
            dma((total,)),
            vmem((RHS, DOF), F32),
            dma((2,)),
            dma,
            pltpu.SemaphoreType.REGULAR,
            pltpu.SemaphoreType.REGULAR((3,)),
        ],
        compiler_params=pltpu.CompilerParams(
            collective_id=0, has_side_effects=True, vmem_limit_bytes=60 * 1024 * 1024
        ),
        name="smooth",
    )(source.reshape(NX, RHS, DOF), *blocks, *tops)
    wide = resid.astype(F32)
    update = lifted.astype(F32) + factor * wide
    remainder = wide - factor * image
    return update.reshape(shape), remainder.reshape(shape)


def solution(mesh):
    field = P("ta", "gz", "yx", None, None, None)
    top = P("ta", "gz", "yx", None, None)
    return jax.shard_map(
        body, mesh=mesh, in_specs=(field,) * 7 + (top,) * 4, out_specs=(field, field), check_vma=False
    )
```

```python
import itertools

import jax
import jax.numpy as jnp
from jax import lax
from jax.experimental import pallas as pl
from jax.experimental.pallas import tpu as pltpu
from jax.sharding import PartitionSpec as P

MESH = pl.DeviceIdType.MESH
F32 = jnp.float32
BF16 = jnp.bfloat16

NX, RHS, DOF = 12, 32, 128
CHUNKS = 2
LOADS = 4
SPAN = NX // CHUNKS
SIZES = {"core": 2, "x": 4, "y": 8, "z": 8}
PHASES = (("z",), ("core", "x", "y"))


def offsets_of(phase):
    every = itertools.product(*(range(SIZES[axis]) for axis in phase))
    return [dict(zip(phase, step)) for step in every if any(step)]


COUNTS = [len(offsets_of(phase)) for phase in PHASES]


def forward(vector, block):
    return lax.dot_general(vector, block, (((1,), (1,)), ((), ())), preferred_element_type=F32)


def adjoint(vector, block):
    return lax.dot_general(vector, block, (((1,), (0,)), ((), ())), preferred_element_type=F32)


def halves(value):
    high = value.astype(BF16)
    low = (value - high.astype(F32)).astype(BF16)
    return jnp.concatenate([high, low], axis=0)


def fold(value):
    return value[:RHS] + value[RHS:]


def kernel(
    src_h, diag_h, lt_h, lz_h, ly_h, lx_h, pro_h, td_h, tt_h, tz_h, ty_h,
    field, image, factor,
    src, diag, links, pro, tops,
    back, field_in, back_in, total,
    coarse, coarse_in, hop_in,
    sum_out, sum_in,
    load_sem,
    coarse_send, coarse_recv, field_send, field_recv, back_send, back_recv,
    sum_send, sum_recv,
    relay_in, relay_send, relay_recv, late_in, met,
):
    ta, gz, yx = lax.axis_index("ta"), lax.axis_index("gz"), lax.axis_index("yx")

    def at(ta_at, gz_at, yx_at):
        return (ta_at, gz_at, yx_at)

    plus = (
        at(lax.rem(ta + 1, 16), gz, yx),
        at(ta, lax.rem(gz + 1, 8), yx),
        at(ta, gz, lax.rem(yx + 1, 4)),
    )
    minus = (
        at(lax.rem(ta + 15, 16), gz, yx),
        at(ta, lax.rem(gz + 7, 8), yx),
        at(ta, gz, lax.rem(yx + 3, 4)),
    )
    here = {
        "core": lax.rem(gz, 2),
        "x": yx,
        "y": (ta // 8) * 4 + gz // 2,
        "z": lax.rem(ta, 8),
    }

    def partner(step):
        place = {
            axis: lax.rem(here[axis] + step.get(axis, 0), size) if step.get(axis, 0) else here[axis]
            for axis, size in SIZES.items()
        }
        return at(
            (place["y"] // 4) * 8 + place["z"],
            lax.rem(place["y"], 4) * 2 + place["core"],
            place["x"],
        )

    y, z = here["y"], here["z"]
    low, high = z == 0, z == 7
    across = partner({"y": 4})
    below, above = partner({"z": 7}), partner({"z": 1})

    pieces = []
    loads = {}

    def load(name, source, target):
        copy = pltpu.make_async_copy(source, target, load_sem.at[len(pieces)])
        copy.start()
        pieces.append(name)
        loads.setdefault(name, []).append(copy)

    def loaded(name):
        for copy in loads[name]:
            copy.wait()

    for part in range(LOADS):
        some = pl.ds(part * (NX // LOADS), NX // LOADS)
        load(("pro", part), pro_h.at[some], pro.at[some])
        load(("src", part), src_h.at[some], src.at[some])
    load("tt", tt_h, tops.at[0])
    load("tz", tz_h, tops.at[1])
    load("ty", ty_h, tops.at[2])
    load("td", td_h, tops.at[3])
    load("lt", lt_h, links.at[0])
    load("lz", lz_h, links.at[1])
    load("ly", ly_h, links.at[2])
    load("lx", lx_h, links.at[3])
    load("diag", diag_h, diag)

    def signal(semaphore, device):
        pl.semaphore_signal(semaphore, inc=1, device_id=device, device_id_type=MESH)

    barrier = pltpu.get_barrier_semaphore()
    for device in [plus[1], minus[1], plus[2], minus[2], partner({"y": 1}), partner({"y": 7})]:
        signal(barrier, device)
    for step in offsets_of(("core", "x")):
        signal(barrier, partner(step))

    @pl.when(low)
    def _():
        signal(barrier, minus[0])
        signal(barrier, below)
        signal(barrier, across)

    @pl.when(jnp.logical_not(low))
    def _():
        signal(barrier, minus[0])

    @pl.when(jnp.logical_not(high))
    def _():
        signal(barrier, plus[0])

    greetings = 13 + jnp.where(high, 3, 2)

    def remote(source, target, send, recv, device):
        return pltpu.make_async_remote_copy(
            src_ref=source, dst_ref=target, send_sem=send, recv_sem=recv,
            device_id=device, device_id_type=MESH,
        )

    restricted = jnp.zeros((RHS, DOF), F32)
    for part in range(LOADS):
        loaded(("pro", part))
        loaded(("src", part))
        for n in range(part * (NX // LOADS), (part + 1) * (NX // LOADS)):
            restricted += adjoint(src[n], pro[n])
    coarse[0] = restricted
    split = halves(restricted)
    for mu, name in enumerate(("tt", "tz", "ty")):
        loaded(name)
        coarse[1 + mu] = fold(adjoint(split, tops[mu]))

    pl.semaphore_wait(barrier, greetings)

    @pl.when(high)
    def _():
        signal(late_in, above)

    signal(met.at[0], partner({"y": 1}))
    signal(met.at[0], partner({"y": 7}))

    @pl.when(jnp.logical_not(low))
    def _():
        signal(met.at[0], below)

    @pl.when(jnp.logical_not(jnp.logical_or(low, high)))
    def _():
        signal(met.at[0], above)

    def value_copy(mu, device):
        return remote(coarse.at[0], coarse_in.at[mu], coarse_send.at[mu], coarse_recv.at[mu], device)

    def hop_copy(mu):
        return remote(
            coarse.at[1 + mu], hop_in.at[mu], coarse_send.at[3 + mu], coarse_recv.at[3 + mu], plus[mu]
        )

    hop_copy(0).start()
    to_relay = remote(coarse.at[0], relay_in, relay_send.at[0], relay_recv, across)
    from_relay = remote(relay_in, coarse_in.at[0], relay_send.at[1], coarse_recv.at[0], below)

    @pl.when(low)
    def _():
        to_relay.start()

    @pl.when(jnp.logical_not(low))
    def _():
        value_copy(0, minus[0]).start()

    for mu in (1, 2):
        value_copy(mu, minus[mu]).start()
        hop_copy(mu).start()

    @pl.when(low)
    def _():
        to_relay.wait_recv()
        pl.semaphore_wait(late_in, 1)
        from_relay.start()
        signal(met.at[0], above)

    loaded("td")
    correction = fold(forward(split, tops[3]))
    for mu in (2, 1, 0):
        value_copy(mu, minus[mu]).wait_recv()
        correction += fold(forward(halves(coarse_in[mu]), tops[mu]))
        hop_copy(mu).wait_recv()
        correction += hop_in[mu]
    coarse_fix = correction.astype(BF16)

    def span(part):
        return pl.ds(part * SPAN, SPAN)

    def field_copy(turn, mu, part):
        return remote(
            field.at[turn, span(part)], field_in.at[turn, mu, span(part)],
            field_send.at[turn, mu, part], field_recv.at[turn, mu, part], minus[mu],
        )

    def back_copy(turn, mu, part):
        return remote(
            back.at[turn, mu, span(part)], back_in.at[turn, mu, span(part)],
            back_send.at[turn, mu, part], back_recv.at[turn, mu, part], plus[mu],
        )

    def sites(part):
        return range(part * SPAN, (part + 1) * SPAN)

    def send_back(turn, mu, part):
        for n in sites(part):
            back[turn, mu, n] = adjoint(field[turn, n], links[mu, n]).astype(BF16)
        back_copy(turn, mu, part).start()

    def local_terms(turn):
        for n in range(NX):
            after, before = (n + 1) % NX, (n - 1) % NX
            value = forward(field[turn, n], diag[n])
            value += forward(field[turn, after], links[3, n])
            value += adjoint(field[turn, before], links[3, before]).astype(BF16).astype(F32)
            total[n] = value

    def arrived(turn, mu, part):
        field_copy(turn, mu, part).wait_recv()
        back_copy(turn, mu, part).wait_recv()

    def hop_terms(turn, mu, n):
        return forward(field_in[turn, mu, n], links[mu, n]) + back_in[turn, mu, n].astype(F32)

    def near_terms(turn):
        for mu in (2, 1):
            for part in range(CHUNKS):
                arrived(turn, mu, part)
                for n in sites(part):
                    total[n] += hop_terms(turn, mu, n)

    def send_near(turn):
        for mu in (1, 2):
            for part in range(CHUNKS):
                field_copy(turn, mu, part).start()
        for mu in (1, 2):
            for part in range(CHUNKS):
                send_back(turn, mu, part)

    loaded("lt")
    for part in range(CHUNKS):
        for n in sites(part):
            field[0, n] = forward(coarse_fix, pro[n]).astype(BF16)
        field_copy(0, 0, part).start()
        send_back(0, 0, part)
    loaded("lz")
    loaded("ly")
    send_near(0)
    pl.semaphore_wait(met.at[0], 2 + jnp.where(jnp.logical_or(low, high), 1, 2))
    for step in ({"y": 2}, {"y": 6}, {"z": 2}, {"z": 6}):
        signal(met.at[1], partner(step))
    loaded("lx")
    loaded("diag")
    local_terms(0)
    near_terms(0)
    for part in range(CHUNKS):
        arrived(0, 0, part)
        for n in sites(part):
            applied = total[n] + hop_terms(0, 0, n)
            field[1, n] = (src[n].astype(F32) - applied).astype(BF16)
        field_copy(1, 0, part).start()
        send_back(1, 0, part)
    send_near(1)

    pl.semaphore_wait(met.at[1], 4)
    signal(met.at[2], across)

    local_terms(1)
    near_terms(1)
    cross = jnp.zeros((RHS, DOF), F32)
    energy = jnp.zeros((RHS, DOF), F32)
    for part in range(CHUNKS):
        arrived(1, 0, part)
        for n in sites(part):
            value = total[n] + hop_terms(1, 0, n)
            image[n] = value
            cross += value * field[1, n].astype(F32)
            energy += value * value

    row = lax.broadcasted_iota(jnp.int32, (RHS, DOF), 0)
    lane = lax.broadcasted_iota(jnp.int32, (RHS, DOF), 1)
    cross_at = jnp.sum(cross, axis=1, keepdims=True)
    energy_at = jnp.sum(energy, axis=1, keepdims=True)
    laid = jnp.where(lane == row, cross_at, jnp.where(lane == row + RHS, energy_at, 0.0))
    sums = jnp.sum(laid, axis=0, keepdims=True)

    pl.semaphore_wait(met.at[2], 1)
    base = 0
    sum_copies = []
    for index, phase in enumerate(PHASES):
        sum_out[index] = sums
        copies = []
        for slot, step in enumerate(offsets_of(phase)):
            copies.append(
                remote(
                    sum_out.at[index], sum_in.at[base + slot],
                    sum_send.at[base + slot], sum_recv.at[base + slot], partner(step),
                )
            )
        for copy in copies:
            copy.start()
        for copy in copies:
            copy.wait_recv()
        for slot in range(len(copies)):
            sums = sums + sum_in[base + slot]
        sum_copies += copies
        base += len(copies)

    wide = jnp.broadcast_to(sums, (RHS, DOF))
    cross_sum = jnp.sum(jnp.where(lane == row, wide, 0.0), axis=1, keepdims=True)
    energy_sum = jnp.sum(jnp.where(lane == row + RHS, wide, 0.0), axis=1, keepdims=True)
    factor[...] = jnp.broadcast_to(cross_sum / (energy_sum + 1e-06), (RHS, DOF))

    @pl.when(low)
    def _():
        to_relay.wait_send()
        from_relay.wait_send()

    @pl.when(jnp.logical_not(low))
    def _():
        value_copy(0, minus[0]).wait_send()

    for mu in range(3):
        if mu:
            value_copy(mu, minus[mu]).wait_send()
        hop_copy(mu).wait_send()
    for copy in sum_copies:
        copy.wait_send()
    for turn in range(2):
        for mu in range(3):
            for part in range(CHUNKS):
                field_copy(turn, mu, part).wait_send()
                back_copy(turn, mu, part).wait_send()


def body(source, diag_block, link_time, link_zaxis, link_yaxis, link_xaxis, prolong,
         top_diag, top_time, top_zaxis, top_yaxis):
    shape = source.shape
    blocks = [
        value.reshape(NX, DOF, DOF)
        for value in (diag_block, link_time, link_zaxis, link_yaxis, link_xaxis, prolong)
    ]
    tops = [value.reshape(DOF, DOF) for value in (top_diag, top_time, top_zaxis, top_yaxis)]
    vmem, dma = pltpu.VMEM, pltpu.SemaphoreType.DMA
    total = sum(COUNTS)
    field, image, factor = pl.pallas_call(
        kernel,
        out_shape=(
            vmem((2, NX, RHS, DOF), BF16),
            vmem((NX, RHS, DOF), F32),
            vmem((RHS, DOF), F32),
        ),
        in_specs=[pl.BlockSpec(memory_space=pltpu.HBM)] * 11,
        out_specs=[pl.BlockSpec(memory_space=pltpu.VMEM)] * 3,
        scratch_shapes=[
            vmem((NX, RHS, DOF), BF16),
            vmem((NX, DOF, DOF), BF16),
            vmem((4, NX, DOF, DOF), BF16),
            vmem((NX, DOF, DOF), BF16),
            vmem((4, DOF, DOF), BF16),
            vmem((2, 3, NX, RHS, DOF), BF16),
            vmem((2, 3, NX, RHS, DOF), BF16),
            vmem((2, 3, NX, RHS, DOF), BF16),
            vmem((NX, RHS, DOF), F32),
            vmem((4, RHS, DOF), F32),
            vmem((3, RHS, DOF), F32),
            vmem((3, RHS, DOF), F32),
            vmem((len(PHASES), 1, DOF), F32),
            vmem((total, 1, DOF), F32),
            dma((2 * LOADS + 9,)),
            dma((6,)),
            dma((6,)),
            dma((2, 3, CHUNKS)),
            dma((2, 3, CHUNKS)),
            dma((2, 3, CHUNKS)),
            dma((2, 3, CHUNKS)),
            dma((total,)),
            dma((total,)),
            vmem((RHS, DOF), F32),
            dma((2,)),
            dma,
            pltpu.SemaphoreType.REGULAR,
            pltpu.SemaphoreType.REGULAR((3,)),
        ],
        compiler_params=pltpu.CompilerParams(
            collective_id=0, has_side_effects=True, vmem_limit_bytes=60 * 1024 * 1024
        ),
        name="smooth",
    )(source.reshape(NX, RHS, DOF), *blocks, *tops)
    wide = field[1].astype(F32)
    update = field[0].astype(F32) + factor * wide
    remainder = wide - factor * image
    return update.reshape(shape), remainder.reshape(shape)


def solution(mesh):
    field = P("ta", "gz", "yx", None, None, None)
    top = P("ta", "gz", "yx", None, None)
    return jax.shard_map(
        body, mesh=mesh, in_specs=(field,) * 7 + (top,) * 4, out_specs=(field, field), check_vma=False
    )
```

```python
import itertools

import jax
import jax.numpy as jnp
from jax import lax
from jax.experimental import pallas as pl
from jax.experimental.pallas import tpu as pltpu
from jax.sharding import PartitionSpec as P

MESH = pl.DeviceIdType.MESH
F32 = jnp.float32
BF16 = jnp.bfloat16

NX, RHS, DOF = 12, 32, 128
CHUNKS = 2
LOADS = 4
SPAN = NX // CHUNKS
SIZES = {"core": 2, "x": 4, "y": 8, "z": 8}
EARLY = 4


def offsets_of(axes):
    every = itertools.product(*(range(SIZES[axis]) for axis in axes))
    return [dict(zip(axes, step)) for step in every if any(step)]


PLANE = [{}] + offsets_of(("core", "x"))


def forward(vector, block):
    return lax.dot_general(vector, block, (((1,), (1,)), ((), ())), preferred_element_type=F32)


def adjoint(vector, block):
    return lax.dot_general(vector, block, (((1,), (0,)), ((), ())), preferred_element_type=F32)


def halves(value):
    high = value.astype(BF16)
    low = (value - high.astype(F32)).astype(BF16)
    return jnp.concatenate([high, low], axis=0)


def fold(value):
    return value[:RHS] + value[RHS:]


def kernel(
    src_h, diag_h, lt_h, lz_h, ly_h, lx_h, pro_h, td_h, tt_h, tz_h, ty_h,
    lifted, resid, image, factor,
    src, diag, links, pro, tops,
    back, field_in, back_in, total,
    coarse, coarse_in, hop_in,
    sum_out, sum_in, direct_in,
    load_sem,
    coarse_send, coarse_recv, field_send, field_recv, back_send, back_recv,
    sum_send, sum_recv,
    direct_send, direct_recv,
    relay_in, relay_send, relay_recv, late_in, met,
):
    field = (lifted, resid)
    ta, gz, yx = lax.axis_index("ta"), lax.axis_index("gz"), lax.axis_index("yx")

    def at(ta_at, gz_at, yx_at):
        return (ta_at, gz_at, yx_at)

    plus = (
        at(lax.rem(ta + 1, 16), gz, yx),
        at(ta, lax.rem(gz + 1, 8), yx),
        at(ta, gz, lax.rem(yx + 1, 4)),
    )
    minus = (
        at(lax.rem(ta + 15, 16), gz, yx),
        at(ta, lax.rem(gz + 7, 8), yx),
        at(ta, gz, lax.rem(yx + 3, 4)),
    )
    here = {
        "core": lax.rem(gz, 2),
        "x": yx,
        "y": (ta // 8) * 4 + gz // 2,
        "z": lax.rem(ta, 8),
    }

    def partner(step):
        place = {
            axis: lax.rem(here[axis] + step[axis], size) if axis in step else here[axis]
            for axis, size in SIZES.items()
        }
        return at(
            (place["y"] // 4) * 8 + place["z"],
            lax.rem(place["y"], 4) * 2 + place["core"],
            place["x"],
        )

    y, z = here["y"], here["z"]
    low, high = z == 0, z == 7
    across = partner({"y": 4})
    below, above = partner({"z": 7}), partner({"z": 1})

    direct_in[...] = jnp.zeros_like(direct_in)
    for slot in range(EARLY):
        sum_in[slot] = jnp.zeros((1, DOF), F32)

    def partner_at(depth, step):
        ta_at, gz_at, yx_at = partner(step)
        return at((ta_at // 8) * 8 + depth, gz_at, yx_at)

    pieces = []
    loads = {}

    def load(name, source, target):
        copy = pltpu.make_async_copy(source, target, load_sem.at[len(pieces)])
        copy.start()
        pieces.append(name)
        loads.setdefault(name, []).append(copy)

    def loaded(name):
        for copy in loads[name]:
            copy.wait()

    for part in range(LOADS):
        some = pl.ds(part * (NX // LOADS), NX // LOADS)
        load(("pro", part), pro_h.at[some], pro.at[some])
        load(("src", part), src_h.at[some], src.at[some])
    load("tt", tt_h, tops.at[0])
    load("tz", tz_h, tops.at[1])
    load("ty", ty_h, tops.at[2])
    load("td", td_h, tops.at[3])
    load("lt", lt_h, links.at[0])
    load("lz", lz_h, links.at[1])
    load("ly", ly_h, links.at[2])
    load("lx", lx_h, links.at[3])
    load("diag", diag_h, diag)

    def signal(semaphore, device):
        pl.semaphore_signal(semaphore, inc=1, device_id=device, device_id_type=MESH)

    barrier = pltpu.get_barrier_semaphore()
    for device in [plus[1], minus[1], plus[2], minus[2], partner({"y": 1}), partner({"y": 7})]:
        signal(barrier, device)
    for step in offsets_of(("core", "x")):
        signal(barrier, partner(step))

    @pl.when(low)
    def _():
        signal(barrier, minus[0])
        signal(barrier, below)
        signal(barrier, across)

    @pl.when(jnp.logical_not(low))
    def _():
        signal(barrier, minus[0])

    @pl.when(jnp.logical_not(high))
    def _():
        signal(barrier, plus[0])

    greetings = 13 + jnp.where(high, 3, 2)

    def remote(source, target, send, recv, device):
        return pltpu.make_async_remote_copy(
            src_ref=source, dst_ref=target, send_sem=send, recv_sem=recv,
            device_id=device, device_id_type=MESH,
        )

    restricted = jnp.zeros((RHS, DOF), F32)
    for part in range(LOADS):
        loaded(("pro", part))
        loaded(("src", part))
        for n in range(part * (NX // LOADS), (part + 1) * (NX // LOADS)):
            restricted += adjoint(src[n], pro[n])
    coarse[0] = restricted
    split = halves(restricted)
    for mu, name in enumerate(("tt", "tz", "ty")):
        loaded(name)
        coarse[1 + mu] = fold(adjoint(split, tops[mu]))

    pl.semaphore_wait(barrier, greetings)

    @pl.when(high)
    def _():
        signal(late_in, above)

    signal(met.at[0], partner({"y": 1}))
    signal(met.at[0], partner({"y": 7}))

    @pl.when(jnp.logical_not(low))
    def _():
        signal(met.at[0], below)

    @pl.when(jnp.logical_not(jnp.logical_or(low, high)))
    def _():
        signal(met.at[0], above)

    def value_copy(mu, device):
        return remote(coarse.at[0], coarse_in.at[mu], coarse_send.at[mu], coarse_recv.at[mu], device)

    def hop_copy(mu):
        return remote(
            coarse.at[1 + mu], hop_in.at[mu], coarse_send.at[3 + mu], coarse_recv.at[3 + mu], plus[mu]
        )

    hop_copy(0).start()
    to_relay = remote(coarse.at[0], relay_in, relay_send.at[0], relay_recv, across)
    from_relay = remote(relay_in, coarse_in.at[0], relay_send.at[1], coarse_recv.at[0], below)

    @pl.when(low)
    def _():
        to_relay.start()

    @pl.when(jnp.logical_not(low))
    def _():
        value_copy(0, minus[0]).start()

    for mu in (1, 2):
        value_copy(mu, minus[mu]).start()
        hop_copy(mu).start()

    @pl.when(low)
    def _():
        to_relay.wait_recv()
        pl.semaphore_wait(late_in, 1)
        from_relay.start()
        signal(met.at[0], above)

    loaded("td")
    correction = fold(forward(split, tops[3]))
    for mu in (2, 1, 0):
        value_copy(mu, minus[mu]).wait_recv()
        correction += fold(forward(halves(coarse_in[mu]), tops[mu]))
        hop_copy(mu).wait_recv()
        correction += hop_in[mu]
    coarse_fix = correction.astype(BF16)

    def span(part):
        return pl.ds(part * SPAN, SPAN)

    def field_copy(turn, mu, part):
        return remote(
            field[turn].at[span(part)], field_in.at[turn, mu, span(part)],
            field_send.at[turn, mu, part], field_recv.at[turn, mu, part], minus[mu],
        )

    def back_copy(turn, mu, part):
        return remote(
            back.at[turn, mu, span(part)], back_in.at[turn, mu, span(part)],
            back_send.at[turn, mu, part], back_recv.at[turn, mu, part], plus[mu],
        )

    def sites(part):
        return range(part * SPAN, (part + 1) * SPAN)

    def send_back(turn, mu, part):
        for n in sites(part):
            back[turn, mu, n] = adjoint(field[turn][n], links[mu, n]).astype(BF16)
        back_copy(turn, mu, part).start()

    def local_terms(turn):
        for n in range(NX):
            after, before = (n + 1) % NX, (n - 1) % NX
            value = forward(field[turn][n], diag[n])
            value += forward(field[turn][after], links[3, n])
            value += adjoint(field[turn][before], links[3, before]).astype(BF16).astype(F32)
            total[n] = value

    def arrived(turn, mu, part):
        field_copy(turn, mu, part).wait_recv()
        back_copy(turn, mu, part).wait_recv()

    def hop_terms(turn, mu, n):
        return forward(field_in[turn, mu, n], links[mu, n]) + back_in[turn, mu, n].astype(F32)

    def near_terms(turn):
        for mu in (2, 1):
            for part in range(CHUNKS):
                arrived(turn, mu, part)
                for n in sites(part):
                    total[n] += hop_terms(turn, mu, n)

    def send_near(turn):
        for mu in (1, 2):
            for part in range(CHUNKS):
                field_copy(turn, mu, part).start()
        for mu in (1, 2):
            for part in range(CHUNKS):
                send_back(turn, mu, part)

    loaded("lt")
    for part in range(CHUNKS):
        for n in sites(part):
            field[0][n] = forward(coarse_fix, pro[n]).astype(BF16)
        field_copy(0, 0, part).start()
        send_back(0, 0, part)
    loaded("lz")
    loaded("ly")
    send_near(0)
    pl.semaphore_wait(met.at[0], 2 + jnp.where(jnp.logical_or(low, high), 1, 2))
    for step in ({"y": 2}, {"y": 6}, {"z": 2}, {"z": 6}):
        signal(met.at[1], partner(step))
    loaded("lx")
    loaded("diag")
    local_terms(0)
    near_terms(0)
    pl.semaphore_wait(met.at[1], 4)
    signal(met.at[2], across)
    for part in range(CHUNKS):
        arrived(0, 0, part)
        for n in sites(part):
            applied = total[n] + hop_terms(0, 0, n)
            field[1][n] = (src[n].astype(F32) - applied).astype(BF16)
        field_copy(1, 0, part).start()
        send_back(1, 0, part)
    send_near(1)

    local_terms(1)
    pl.semaphore_wait(met.at[2], 1)

    @pl.when(z < EARLY)
    def _():
        signal(met.at[3], partner_at(7, {}))

    near_terms(1)
    cross = jnp.zeros((RHS, DOF), F32)
    energy = jnp.zeros((RHS, DOF), F32)
    for part in range(CHUNKS):
        arrived(1, 0, part)
        for n in sites(part):
            value = total[n] + hop_terms(1, 0, n)
            image[n] = value
            cross += value * field[1][n].astype(F32)
            energy += value * value

    row = lax.broadcasted_iota(jnp.int32, (RHS, DOF), 0)
    lane = lax.broadcasted_iota(jnp.int32, (RHS, DOF), 1)
    cross_at = jnp.sum(cross, axis=1, keepdims=True)
    energy_at = jnp.sum(energy, axis=1, keepdims=True)
    laid = jnp.where(lane == row, cross_at, jnp.where(lane == row + RHS, energy_at, 0.0))
    sums = jnp.sum(laid, axis=0, keepdims=True)

    own = sum_out.at[0]
    sum_out[0] = sums

    def own_copy(slot, depth, step):
        return remote(
            own, direct_in.at[slot], direct_send.at[depth], direct_recv, partner_at(depth, step)
        )

    @pl.when(high)
    def _():
        pl.semaphore_wait(met.at[3], EARLY)
        for depth in range(EARLY):

            def spread(turned, carry):
                along = lax.rem(turned + 4, 8)
                for slot, step in enumerate(PLANE):
                    own_copy(along * len(PLANE) + slot, depth, {**step, "y": along}).start()
                return carry

            lax.fori_loop(0, 8, spread, 0)

    def along_copy(slot):
        return remote(
            own, sum_in.at[slot], sum_send.at[slot], sum_recv.at[slot], partner({"z": slot + 1})
        )

    def some(slot, hidden, act):
        if slot < EARLY:
            pl.when(jnp.logical_not(hidden))(act)
        else:
            act()

    for slot in range(7):
        some(slot, high, lambda: along_copy(slot).start())
    for slot in range(7):
        some(slot, z == slot, lambda: along_copy(slot).wait_recv())
    for slot in range(7):
        sums = sums + sum_in[slot]

    sum_out[1] = sums
    plane_copies = [
        remote(sum_out.at[1], sum_in.at[7 + slot], sum_send.at[7 + slot], sum_recv.at[7 + slot], partner(step))
        for slot, step in enumerate(offsets_of(("core", "x", "y")))
    ]
    for copy in plane_copies:
        copy.start()
    for copy in plane_copies:
        copy.wait_recv()
    sums = sums + jnp.sum(sum_in[7:], axis=0)

    @pl.when(z < EARLY)
    def _():
        pltpu.make_async_copy(direct_in, direct_in, direct_recv).wait()

    sums = sums + jnp.sum(direct_in[...], axis=0)

    wide = jnp.broadcast_to(sums, (RHS, DOF))
    cross_sum = jnp.sum(jnp.where(lane == row, wide, 0.0), axis=1, keepdims=True)
    energy_sum = jnp.sum(jnp.where(lane == row + RHS, wide, 0.0), axis=1, keepdims=True)
    factor[...] = jnp.broadcast_to(cross_sum / (energy_sum + 1e-06), (RHS, DOF))

    @pl.when(low)
    def _():
        to_relay.wait_send()
        from_relay.wait_send()

    @pl.when(jnp.logical_not(low))
    def _():
        value_copy(0, minus[0]).wait_send()

    for mu in range(3):
        if mu:
            value_copy(mu, minus[mu]).wait_send()
        hop_copy(mu).wait_send()
    for slot in range(7):
        some(slot, high, lambda: along_copy(slot).wait_send())
    for copy in plane_copies:
        copy.wait_send()

    @pl.when(high)
    def _():
        for depth in range(EARLY):
            pltpu.make_async_copy(direct_in, direct_in, direct_send.at[depth]).wait()

    for turn in range(2):
        for mu in range(3):
            for part in range(CHUNKS):
                field_copy(turn, mu, part).wait_send()
                back_copy(turn, mu, part).wait_send()


def body(source, diag_block, link_time, link_zaxis, link_yaxis, link_xaxis, prolong,
         top_diag, top_time, top_zaxis, top_yaxis):
    shape = source.shape
    blocks = [
        value.reshape(NX, DOF, DOF)
        for value in (diag_block, link_time, link_zaxis, link_yaxis, link_xaxis, prolong)
    ]
    tops = [value.reshape(DOF, DOF) for value in (top_diag, top_time, top_zaxis, top_yaxis)]
    vmem, dma = pltpu.VMEM, pltpu.SemaphoreType.DMA
    total = 7 + 63
    lifted, resid, image, factor = pl.pallas_call(
        kernel,
        out_shape=(
            vmem((NX, RHS, DOF), BF16),
            vmem((NX, RHS, DOF), BF16),
            vmem((NX, RHS, DOF), F32),
            vmem((RHS, DOF), F32),
        ),
        in_specs=[pl.BlockSpec(memory_space=pltpu.HBM)] * 11,
        out_specs=[pl.BlockSpec(memory_space=pltpu.VMEM)] * 4,
        scratch_shapes=[
            vmem((NX, RHS, DOF), BF16),
            vmem((NX, DOF, DOF), BF16),
            vmem((4, NX, DOF, DOF), BF16),
            vmem((NX, DOF, DOF), BF16),
            vmem((4, DOF, DOF), BF16),
            vmem((2, 3, NX, RHS, DOF), BF16),
            vmem((2, 3, NX, RHS, DOF), BF16),
            vmem((2, 3, NX, RHS, DOF), BF16),
            vmem((NX, RHS, DOF), F32),
            vmem((4, RHS, DOF), F32),
            vmem((3, RHS, DOF), F32),
            vmem((3, RHS, DOF), F32),
            vmem((2, 1, DOF), F32),
            vmem((total, 1, DOF), F32),
            vmem((64, 1, DOF), F32),
            dma((2 * LOADS + 9,)),
            dma((6,)),
            dma((6,)),
            dma((2, 3, CHUNKS)),
            dma((2, 3, CHUNKS)),
            dma((2, 3, CHUNKS)),
            dma((2, 3, CHUNKS)),
            dma((total,)),
            dma((total,)),
            dma((EARLY,)),
            dma,
            vmem((RHS, DOF), F32),
            dma((2,)),
            dma,
            pltpu.SemaphoreType.REGULAR,
            pltpu.SemaphoreType.REGULAR((4,)),
        ],
        compiler_params=pltpu.CompilerParams(
            collective_id=0, has_side_effects=True, vmem_limit_bytes=60 * 1024 * 1024
        ),
        name="smooth",
    )(source.reshape(NX, RHS, DOF), *blocks, *tops)
    wide = resid.astype(F32)
    update = lifted.astype(F32) + factor * wide
    remainder = wide - factor * image
    return update.reshape(shape), remainder.reshape(shape)


def solution(mesh):
    field = P("ta", "gz", "yx", None, None, None)
    top = P("ta", "gz", "yx", None, None)
    return jax.shard_map(
        body, mesh=mesh, in_specs=(field,) * 7 + (top,) * 4, out_specs=(field, field), check_vma=False
    )
```

```python
import itertools

import jax
import jax.numpy as jnp
from jax import lax
from jax.experimental import pallas as pl
from jax.experimental.pallas import tpu as pltpu
from jax.sharding import PartitionSpec as P

MESH = pl.DeviceIdType.MESH
F32 = jnp.float32
BF16 = jnp.bfloat16

NX, RHS, DOF = 12, 32, 128
CHUNKS = 2
LOADS = 2
SPAN = NX // CHUNKS
SIZES = {"core": 2, "x": 4, "y": 8, "z": 8}
EARLY = 4


def offsets_of(axes):
    every = itertools.product(*(range(SIZES[axis]) for axis in axes))
    return [dict(zip(axes, step)) for step in every if any(step)]


PLANE = [{}] + offsets_of(("core", "x"))


def forward(vector, block):
    return lax.dot_general(vector, block, (((1,), (1,)), ((), ())), preferred_element_type=F32)


def adjoint(vector, block):
    return lax.dot_general(vector, block, (((1,), (0,)), ((), ())), preferred_element_type=F32)


def halves(value):
    high = value.astype(BF16)
    low = (value - high.astype(F32)).astype(BF16)
    return jnp.concatenate([high, low], axis=0)


def fold(value):
    return value[:RHS] + value[RHS:]


def kernel(
    src_h, diag_h, lt_h, lz_h, ly_h, lx_h, pro_h, td_h, tt_h, tz_h, ty_h,
    lifted, resid, image, factor,
    src, diag, links, pro, tops,
    back, field_in, back_in, total,
    coarse, coarse_in, hop_in,
    sum_out, sum_in, direct_in,
    load_sem, coarse_send, coarse_recv, field_send, near_recv, wrap_recv,
    sum_send, sum_recv, direct_send, direct_recv,
    relay_in, relay_recv, late_in, met,
):
    field = (lifted, resid)
    ta, gz, yx = lax.axis_index("ta"), lax.axis_index("gz"), lax.axis_index("yx")

    def at(ta_at, gz_at, yx_at):
        return (ta_at, gz_at, yx_at)

    plus = (
        at(lax.rem(ta + 1, 16), gz, yx),
        at(ta, lax.rem(gz + 1, 8), yx),
        at(ta, gz, lax.rem(yx + 1, 4)),
    )
    minus = (
        at(lax.rem(ta + 15, 16), gz, yx),
        at(ta, lax.rem(gz + 7, 8), yx),
        at(ta, gz, lax.rem(yx + 3, 4)),
    )
    here = {
        "core": lax.rem(gz, 2),
        "x": yx,
        "y": (ta // 8) * 4 + gz // 2,
        "z": lax.rem(ta, 8),
    }

    def partner(step):
        place = {
            axis: lax.rem(here[axis] + step[axis], size) if axis in step else here[axis]
            for axis, size in SIZES.items()
        }
        return at(
            (place["y"] // 4) * 8 + place["z"],
            lax.rem(place["y"], 4) * 2 + place["core"],
            place["x"],
        )

    y, z = here["y"], here["z"]
    low, high = z == 0, z == 7
    across = partner({"y": 4})
    below, above = partner({"z": 7}), partner({"z": 1})

    direct_in[...] = jnp.zeros_like(direct_in)
    for slot in range(EARLY):
        sum_in[slot] = jnp.zeros((1, DOF), F32)

    def partner_at(depth, step):
        ta_at, gz_at, yx_at = partner(step)
        return at((ta_at // 8) * 8 + depth, gz_at, yx_at)

    def taken(ref, semaphore):
        pltpu.make_async_copy(ref, ref, semaphore).wait()

    def load(source, target, slot):
        pltpu.make_async_copy(source, target, load_sem.at[slot]).start()

    for part in range(LOADS):
        some = pl.ds(part * (NX // LOADS), NX // LOADS)
        load(pro_h.at[some], pro.at[some], 2 * part)
        load(src_h.at[some], src.at[some], 2 * part + 1)
    for slot, source in enumerate((tt_h, tz_h, ty_h, td_h)):
        load(source, tops.at[slot], 2 * LOADS)
    for slot, source in enumerate((lt_h, lz_h, ly_h, lx_h)):
        load(source, links.at[slot], 2 * LOADS + 1)
    load(diag_h, diag, 2 * LOADS + 2)

    def signal(semaphore, device):
        pl.semaphore_signal(semaphore, inc=1, device_id=device, device_id_type=MESH)

    barrier = pltpu.get_barrier_semaphore()
    for device in [plus[1], minus[1], plus[2], minus[2], partner({"y": 1}), partner({"y": 7})]:
        signal(barrier, device)
    for step in offsets_of(("core", "x")):
        signal(barrier, partner(step))

    @pl.when(low)
    def _():
        signal(barrier, minus[0])
        signal(barrier, below)
        signal(barrier, across)

    @pl.when(jnp.logical_not(low))
    def _():
        signal(barrier, minus[0])

    @pl.when(jnp.logical_not(high))
    def _():
        signal(barrier, plus[0])

    greetings = 13 + jnp.where(high, 3, 2)

    def remote(source, target, send, recv, device):
        return pltpu.make_async_remote_copy(
            src_ref=source, dst_ref=target, send_sem=send, recv_sem=recv,
            device_id=device, device_id_type=MESH,
        )

    restricted = jnp.zeros((RHS, DOF), F32)
    for part in range(LOADS):
        some = pl.ds(part * (NX // LOADS), NX // LOADS)
        taken(pro.at[some], load_sem.at[2 * part])
        taken(src.at[some], load_sem.at[2 * part + 1])
        for n in range(part * (NX // LOADS), (part + 1) * (NX // LOADS)):
            restricted += adjoint(src[n], pro[n])
    coarse[0] = restricted
    split = halves(restricted)
    taken(tops, load_sem.at[2 * LOADS])
    coarse[1] = fold(adjoint(split, tops[0]))

    pl.semaphore_wait(barrier, greetings)

    def value_copy(mu, device):
        return remote(coarse.at[0], coarse_in.at[mu], coarse_send, coarse_recv.at[min(mu, 1)], device)

    def hop_copy(mu):
        return remote(coarse.at[1 + mu], hop_in.at[mu], coarse_send, coarse_recv.at[min(mu, 1)], plus[mu])

    hop_copy(0).start()
    to_relay = remote(coarse.at[0], relay_in, coarse_send, relay_recv, across)
    from_relay = remote(relay_in, coarse_in.at[0], coarse_send, coarse_recv.at[0], below)

    @pl.when(low)
    def _():
        to_relay.start()

    @pl.when(jnp.logical_not(low))
    def _():
        value_copy(0, minus[0]).start()

    for mu in (1, 2):
        value_copy(mu, minus[mu]).start()

    @pl.when(high)
    def _():
        signal(late_in, above)

    signal(met.at[0], partner({"y": 1}))
    signal(met.at[0], partner({"y": 7}))

    @pl.when(jnp.logical_not(low))
    def _():
        signal(met.at[0], below)

    @pl.when(jnp.logical_not(jnp.logical_or(low, high)))
    def _():
        signal(met.at[0], above)

    for mu in (1, 2):
        coarse[1 + mu] = fold(adjoint(split, tops[mu]))
        hop_copy(mu).start()

    @pl.when(low)
    def _():
        to_relay.wait_recv()
        pl.semaphore_wait(late_in, 1)
        from_relay.start()
        signal(met.at[0], above)

    correction = fold(forward(split, tops[3]))
    taken(total.at[pl.ds(0, 4)], coarse_recv.at[1])
    for mu in (2, 1):
        correction += fold(forward(halves(coarse_in[mu]), tops[mu])) + hop_in[mu]
    taken(total.at[pl.ds(0, 2)], coarse_recv.at[0])
    correction += fold(forward(halves(coarse_in[0]), tops[0])) + hop_in[0]
    coarse_fix = correction.astype(BF16)

    def span(part):
        return pl.ds(part * SPAN, SPAN)

    def landing(turn, mu, part):
        return near_recv.at[turn, mu - 1] if mu else wrap_recv.at[turn, part]

    def field_copy(turn, mu, part):
        return remote(
            field[turn].at[span(part)], field_in.at[turn, mu, span(part)],
            field_send, landing(turn, mu, part), minus[mu],
        )

    def back_copy(turn, mu, part):
        return remote(
            back.at[turn, mu, span(part)], back_in.at[turn, mu, span(part)],
            field_send, landing(turn, mu, part), plus[mu],
        )

    def sites(part):
        return range(part * SPAN, (part + 1) * SPAN)

    def send_back(turn, mu, part):
        for n in sites(part):
            back[turn, mu, n] = adjoint(field[turn][n], links[mu, n]).astype(BF16)
        back_copy(turn, mu, part).start()

    def local_terms(turn):
        for n in range(NX):
            after, before = (n + 1) % NX, (n - 1) % NX
            value = forward(field[turn][n], diag[n])
            value += forward(field[turn][after], links[3, n])
            value += adjoint(field[turn][before], links[3, before]).astype(BF16).astype(F32)
            total[n] = value

    def hop_terms(turn, mu, n):
        return forward(field_in[turn, mu, n], links[mu, n]) + back_in[turn, mu, n].astype(F32)

    def near_terms(turn):
        for mu in (2, 1):
            taken(field_in.at[turn, pl.ds(0, 2)], near_recv.at[turn, mu - 1])
            for n in range(NX):
                total[n] += hop_terms(turn, mu, n)

    def send_wrap(turn, part):
        @pl.when(low)
        def _():
            field_copy(turn, 0, part).start()

        for n in sites(part):
            back[turn, 0, n] = adjoint(field[turn][n], links[0, n]).astype(BF16)

        @pl.when(high)
        def _():
            back_copy(turn, 0, part).start()

    def send_rest(turn):
        for mu in (1, 2):
            for part in range(CHUNKS):
                field_copy(turn, mu, part).start()
        for mu in (1, 2):
            for part in range(CHUNKS):
                send_back(turn, mu, part)
        for part in range(CHUNKS):

            @pl.when(jnp.logical_not(low))
            def _():
                field_copy(turn, 0, part).start()

            @pl.when(jnp.logical_not(high))
            def _():
                back_copy(turn, 0, part).start()

    taken(links, load_sem.at[2 * LOADS + 1])
    for part in range(CHUNKS):
        for n in sites(part):
            field[0][n] = forward(coarse_fix, pro[n]).astype(BF16)
        send_wrap(0, part)
    send_rest(0)
    pl.semaphore_wait(met.at[0], 2 + jnp.where(jnp.logical_or(low, high), 1, 2))
    for step in ({"y": 2}, {"y": 6}, {"z": 2}, {"z": 6}):
        signal(met.at[1], partner(step))
    taken(diag, load_sem.at[2 * LOADS + 2])
    local_terms(0)
    near_terms(0)
    pl.semaphore_wait(met.at[1], 4)
    signal(met.at[2], across)
    for part in range(CHUNKS):
        taken(field_in.at[0, 0, pl.ds(0, 2 * SPAN)], wrap_recv.at[0, part])
        for n in sites(part):
            applied = total[n] + hop_terms(0, 0, n)
            field[1][n] = (src[n].astype(F32) - applied).astype(BF16)
        send_wrap(1, part)
    send_rest(1)

    local_terms(1)
    pl.semaphore_wait(met.at[2], 1)

    @pl.when(z < EARLY)
    def _():
        signal(met.at[3], partner_at(7, {}))

    near_terms(1)
    cross = jnp.zeros((RHS, DOF), F32)
    energy = jnp.zeros((RHS, DOF), F32)
    for part in range(CHUNKS):
        taken(field_in.at[1, 0, pl.ds(0, 2 * SPAN)], wrap_recv.at[1, part])
        for n in sites(part):
            value = total[n] + hop_terms(1, 0, n)
            image[n] = value
            cross += value * field[1][n].astype(F32)
            energy += value * value

    row = lax.broadcasted_iota(jnp.int32, (RHS, DOF), 0)
    lane = lax.broadcasted_iota(jnp.int32, (RHS, DOF), 1)
    cross_at = jnp.sum(cross, axis=1, keepdims=True)
    energy_at = jnp.sum(energy, axis=1, keepdims=True)
    laid = jnp.where(lane == row, cross_at, jnp.where(lane == row + RHS, energy_at, 0.0))
    sums = jnp.sum(laid, axis=0, keepdims=True)

    own = sum_out.at[0]
    sum_out[0] = sums

    def own_copy(slot, depth, step):
        return remote(
            own, direct_in.at[slot], direct_send, direct_recv, partner_at(depth, step)
        )

    @pl.when(high)
    def _():
        pl.semaphore_wait(met.at[3], EARLY)
        for depth in range(EARLY):

            def spread(turned, carry):
                along = lax.rem(turned + 4, 8)
                for slot, step in enumerate(PLANE):
                    own_copy(along * len(PLANE) + slot, depth, {**step, "y": along}).start()
                return carry

            lax.fori_loop(0, 8, spread, 0)

    def along_copy(slot):
        return remote(
            own, sum_in.at[slot], sum_send, sum_recv.at[0], partner({"z": slot + 1})
        )

    @pl.when(jnp.logical_not(high))
    def _():
        for slot in range(EARLY):
            along_copy(slot).start()

    for slot in range(EARLY, 7):
        along_copy(slot).start()

    @pl.when(z < EARLY)
    def _():
        taken(sum_in.at[pl.ds(0, 6)], sum_recv.at[0])

    @pl.when(z >= EARLY)
    def _():
        taken(sum_in.at[pl.ds(0, 7)], sum_recv.at[0])

    for slot in range(7):
        sums = sums + sum_in[slot]

    sum_out[1] = sums
    plane_copies = [
        remote(sum_out.at[1], sum_in.at[7 + slot], sum_send, sum_recv.at[1], partner(step))
        for slot, step in enumerate(offsets_of(("core", "x", "y")))
    ]
    for copy in plane_copies:
        copy.start()
    taken(sum_in.at[pl.ds(7, 63)], sum_recv.at[1])
    sums = sums + jnp.sum(sum_in[7:], axis=0)

    @pl.when(low)
    def _():
        taken(total.at[pl.ds(0, 7)], coarse_send)

    @pl.when(jnp.logical_not(low))
    def _():
        taken(total.at[pl.ds(0, 6)], coarse_send)

    taken(links.at[pl.ds(0, 3)], field_send)

    @pl.when(high)
    def _():
        taken(sum_in.at[pl.ds(0, 70 - EARLY)], sum_send)
        taken(total.at[pl.ds(0, 2 * EARLY)], direct_send)

    @pl.when(jnp.logical_not(high))
    def _():
        taken(sum_in, sum_send)

    @pl.when(z < EARLY)
    def _():
        taken(direct_in, direct_recv)

    sums = sums + jnp.sum(direct_in[...], axis=0)

    wide = jnp.broadcast_to(sums, (RHS, DOF))
    cross_sum = jnp.sum(jnp.where(lane == row, wide, 0.0), axis=1, keepdims=True)
    energy_sum = jnp.sum(jnp.where(lane == row + RHS, wide, 0.0), axis=1, keepdims=True)
    factor[...] = jnp.broadcast_to(cross_sum / (energy_sum + 1e-06), (RHS, DOF))


def body(source, diag_block, link_time, link_zaxis, link_yaxis, link_xaxis, prolong,
         top_diag, top_time, top_zaxis, top_yaxis):
    shape = source.shape
    blocks = [
        value.reshape(NX, DOF, DOF)
        for value in (diag_block, link_time, link_zaxis, link_yaxis, link_xaxis, prolong)
    ]
    tops = [value.reshape(DOF, DOF) for value in (top_diag, top_time, top_zaxis, top_yaxis)]
    vmem, dma = pltpu.VMEM, pltpu.SemaphoreType.DMA
    total = 7 + 63
    lifted, resid, image, factor = pl.pallas_call(
        kernel,
        out_shape=(
            vmem((NX, RHS, DOF), BF16),
            vmem((NX, RHS, DOF), BF16),
            vmem((NX, RHS, DOF), F32),
            vmem((RHS, DOF), F32),
        ),
        in_specs=[pl.BlockSpec(memory_space=pltpu.HBM)] * 11,
        out_specs=[pl.BlockSpec(memory_space=pltpu.VMEM)] * 4,
        scratch_shapes=[
            vmem((NX, RHS, DOF), BF16),
            vmem((NX, DOF, DOF), BF16),
            vmem((4, NX, DOF, DOF), BF16),
            vmem((NX, DOF, DOF), BF16),
            vmem((4, DOF, DOF), BF16),
            vmem((2, 3, NX, RHS, DOF), BF16),
            vmem((2, 3, NX, RHS, DOF), BF16),
            vmem((2, 3, NX, RHS, DOF), BF16),
            vmem((NX, RHS, DOF), F32),
            vmem((4, RHS, DOF), F32),
            vmem((3, RHS, DOF), F32),
            vmem((3, RHS, DOF), F32),
            vmem((2, 1, DOF), F32),
            vmem((total, 1, DOF), F32),
            vmem((64, 1, DOF), F32),
            dma((2 * LOADS + 3,)),
            dma,
            dma((2,)),
            dma,
            dma((2, 2)),
            dma((2, CHUNKS)),
            dma,
            dma((2,)),
            dma,
            dma,
            vmem((RHS, DOF), F32),
            dma,
            pltpu.SemaphoreType.REGULAR,
            pltpu.SemaphoreType.REGULAR((4,)),
        ],
        compiler_params=pltpu.CompilerParams(
            collective_id=0, has_side_effects=True, vmem_limit_bytes=60 * 1024 * 1024
        ),
        name="smooth",
    )(source.reshape(NX, RHS, DOF), *blocks, *tops)
    wide = resid.astype(F32)
    update = lifted.astype(F32) + factor * wide
    remainder = wide - factor * image
    return update.reshape(shape), remainder.reshape(shape)


def solution(mesh):
    field = P("ta", "gz", "yx", None, None, None)
    top = P("ta", "gz", "yx", None, None)
    return jax.shard_map(
        body, mesh=mesh, in_specs=(field,) * 7 + (top,) * 4, out_specs=(field, field), check_vma=False
    )
```

```python
import itertools

import jax
import jax.numpy as jnp
from jax import lax
from jax.experimental import pallas as pl
from jax.experimental.pallas import tpu as pltpu
from jax.sharding import PartitionSpec as P

MESH = pl.DeviceIdType.MESH
F32 = jnp.float32
BF16 = jnp.bfloat16

NX, RHS, DOF = 12, 32, 128
CHUNKS = 2
LOADS = 2
SPAN = NX // CHUNKS
SIZES = {"core": 2, "x": 4, "y": 8, "z": 8}
EARLY = 4


def offsets_of(axes):
    every = itertools.product(*(range(SIZES[axis]) for axis in axes))
    return [dict(zip(axes, step)) for step in every if any(step)]


PLANE = [{}] + offsets_of(("core", "x"))


def forward(vector, block):
    return lax.dot_general(vector, block, (((1,), (1,)), ((), ())), preferred_element_type=F32)


def adjoint(vector, block):
    return lax.dot_general(vector, block, (((1,), (0,)), ((), ())), preferred_element_type=F32)


def halves(value):
    high = value.astype(BF16)
    low = (value - high.astype(F32)).astype(BF16)
    return jnp.concatenate([high, low], axis=0)


def fold(value):
    return value[:RHS] + value[RHS:]


def kernel(
    src_h, diag_h, lt_h, lz_h, ly_h, lx_h, pro_h, td_h, tt_h, tz_h, ty_h,
    lifted, resid, image, factor,
    src, diag, links, pro, tops,
    back, field_in, back_in, total,
    coarse, coarse_in, hop_in,
    sum_out, sum_in, direct_in,
    load_sem, coarse_send, coarse_recv, field_send, wrap_send, near_recv, wrap_recv,
    sum_send, sum_recv, direct_send, direct_recv,
    relay_in, relay_recv, late_in, met,
):
    field = (lifted, resid)
    ta, gz, yx = lax.axis_index("ta"), lax.axis_index("gz"), lax.axis_index("yx")

    def at(ta_at, gz_at, yx_at):
        return (ta_at, gz_at, yx_at)

    plus = (
        at(lax.rem(ta + 1, 16), gz, yx),
        at(ta, lax.rem(gz + 1, 8), yx),
        at(ta, gz, lax.rem(yx + 1, 4)),
    )
    minus = (
        at(lax.rem(ta + 15, 16), gz, yx),
        at(ta, lax.rem(gz + 7, 8), yx),
        at(ta, gz, lax.rem(yx + 3, 4)),
    )
    here = {
        "core": lax.rem(gz, 2),
        "x": yx,
        "y": (ta // 8) * 4 + gz // 2,
        "z": lax.rem(ta, 8),
    }

    def partner(step):
        place = {
            axis: lax.rem(here[axis] + step[axis], size) if axis in step else here[axis]
            for axis, size in SIZES.items()
        }
        return at(
            (place["y"] // 4) * 8 + place["z"],
            lax.rem(place["y"], 4) * 2 + place["core"],
            place["x"],
        )

    y, z = here["y"], here["z"]
    low, high = z == 0, z == 7
    across = partner({"y": 4})
    below, above = partner({"z": 7}), partner({"z": 1})

    direct_in[...] = jnp.zeros_like(direct_in)
    for slot in range(EARLY):
        sum_in[slot] = jnp.zeros((1, DOF), F32)

    def partner_at(depth, step):
        ta_at, gz_at, yx_at = partner(step)
        return at((ta_at // 8) * 8 + depth, gz_at, yx_at)

    def taken(ref, semaphore):
        pltpu.make_async_copy(ref, ref, semaphore).wait()

    def load(source, target, slot):
        pltpu.make_async_copy(source, target, load_sem.at[slot]).start()

    for part in range(LOADS):
        some = pl.ds(part * (NX // LOADS), NX // LOADS)
        load(pro_h.at[some], pro.at[some], 2 * part)
        load(src_h.at[some], src.at[some], 2 * part + 1)
    for slot, source in enumerate((tt_h, tz_h, ty_h, td_h)):
        load(source, tops.at[slot], 2 * LOADS)

    def signal(semaphore, device):
        pl.semaphore_signal(semaphore, inc=1, device_id=device, device_id_type=MESH)

    barrier = pltpu.get_barrier_semaphore()
    for device in [plus[1], minus[1], plus[2], minus[2], partner({"y": 1}), partner({"y": 7})]:
        signal(barrier, device)
    for step in offsets_of(("core", "x")):
        signal(barrier, partner(step))

    @pl.when(low)
    def _():
        signal(barrier, minus[0])
        signal(barrier, below)
        signal(barrier, across)

    @pl.when(jnp.logical_not(low))
    def _():
        signal(barrier, minus[0])

    @pl.when(jnp.logical_not(high))
    def _():
        signal(barrier, plus[0])

    greetings = 13 + jnp.where(high, 3, 2)

    def remote(source, target, send, recv, device):
        return pltpu.make_async_remote_copy(
            src_ref=source, dst_ref=target, send_sem=send, recv_sem=recv,
            device_id=device, device_id_type=MESH,
        )

    restricted = jnp.zeros((RHS, DOF), F32)
    for part in range(LOADS):
        some = pl.ds(part * (NX // LOADS), NX // LOADS)
        taken(pro.at[some], load_sem.at[2 * part])
        taken(src.at[some], load_sem.at[2 * part + 1])
        for n in range(part * (NX // LOADS), (part + 1) * (NX // LOADS)):
            restricted += adjoint(src[n], pro[n])
    coarse[0] = restricted.astype(BF16)
    split = halves(restricted)
    for slot, source in enumerate((lt_h, lz_h, ly_h, lx_h)):
        load(source, links.at[slot], 2 * LOADS + 1)
    load(diag_h, diag, 2 * LOADS + 2)

    taken(tops, load_sem.at[2 * LOADS])
    coarse[1] = fold(adjoint(split, tops[0])).astype(BF16)

    pl.semaphore_wait(barrier, greetings)

    def value_copy(mu, device):
        return remote(coarse.at[0], coarse_in.at[mu], coarse_send, coarse_recv.at[min(mu, 1)], device)

    def hop_copy(mu):
        return remote(coarse.at[1 + mu], hop_in.at[mu], coarse_send, coarse_recv.at[min(mu, 1)], plus[mu])

    hop_copy(0).start()
    to_relay = remote(coarse.at[0], relay_in, coarse_send, relay_recv, across)
    from_relay = remote(relay_in, coarse_in.at[0], coarse_send, coarse_recv.at[0], below)

    @pl.when(low)
    def _():
        to_relay.start()

    @pl.when(jnp.logical_not(low))
    def _():
        value_copy(0, minus[0]).start()

    for mu in (1, 2):
        value_copy(mu, minus[mu]).start()

    @pl.when(high)
    def _():
        signal(late_in, above)

    signal(met.at[0], partner({"y": 1}))
    signal(met.at[0], partner({"y": 7}))

    @pl.when(jnp.logical_not(low))
    def _():
        signal(met.at[0], below)

    @pl.when(jnp.logical_not(jnp.logical_or(low, high)))
    def _():
        signal(met.at[0], above)

    for mu in (1, 2):
        coarse[1 + mu] = fold(adjoint(split, tops[mu])).astype(BF16)
        hop_copy(mu).start()

    @pl.when(low)
    def _():
        to_relay.wait_recv()
        pl.semaphore_wait(late_in, 1)
        from_relay.start()
        signal(met.at[0], above)

    correction = fold(forward(split, tops[3]))
    taken(back.at[0, 0, pl.ds(0, 4)], coarse_recv.at[1])
    for mu in (2, 1):
        correction += forward(coarse_in[mu], tops[mu]) + hop_in[mu].astype(F32)
    taken(back.at[0, 0, pl.ds(0, 2)], coarse_recv.at[0])
    correction += forward(coarse_in[0], tops[0]) + hop_in[0].astype(F32)
    coarse_fix = correction.astype(BF16)

    def span(part):
        return pl.ds(part * SPAN, SPAN)

    def landing(turn, mu, part):
        return near_recv.at[turn, mu - 1] if mu else wrap_recv.at[turn, part]

    def field_copy(turn, mu, part):
        return remote(
            field[turn].at[span(part)], field_in.at[turn, mu, span(part)],
            wrap_send if (turn, mu) == (1, 0) else field_send, landing(turn, mu, part), minus[mu],
        )

    def back_copy(turn, mu, part):
        return remote(
            back.at[turn, mu, span(part)], back_in.at[turn, mu, span(part)],
            field_send, landing(turn, mu, part), plus[mu],
        )

    def sites(part):
        return range(part * SPAN, (part + 1) * SPAN)

    def send_back(turn, mu, part):
        for n in sites(part):
            back[turn, mu, n] = adjoint(field[turn][n], links[mu, n]).astype(BF16)
        back_copy(turn, mu, part).start()

    def local_terms(turn):
        for n in range(NX):
            after, before = (n + 1) % NX, (n - 1) % NX
            value = forward(field[turn][n], diag[n])
            value += forward(field[turn][after], links[3, n])
            value += adjoint(field[turn][before], links[3, before]).astype(BF16).astype(F32)
            total[n] = value

    def hop_terms(turn, mu, n):
        return forward(field_in[turn, mu, n], links[mu, n]) + back_in[turn, mu, n].astype(F32)

    def near_terms(turn):
        for mu in (2, 1):
            taken(field_in.at[turn, pl.ds(0, 2)], near_recv.at[turn, mu - 1])
            for n in range(NX):
                total[n] += hop_terms(turn, mu, n)

    def send_wrap(turn, part):
        @pl.when(low)
        def _():
            field_copy(turn, 0, part).start()

        for n in sites(part):
            back[turn, 0, n] = adjoint(field[turn][n], links[0, n]).astype(BF16)

        @pl.when(high)
        def _():
            back_copy(turn, 0, part).start()

    def send_rest(turn):
        for mu in (1, 2):
            for part in range(CHUNKS):
                field_copy(turn, mu, part).start()
        for mu in (1, 2):
            for part in range(CHUNKS):
                send_back(turn, mu, part)
        for part in range(CHUNKS):

            @pl.when(jnp.logical_not(low))
            def _():
                field_copy(turn, 0, part).start()

            @pl.when(jnp.logical_not(high))
            def _():
                back_copy(turn, 0, part).start()

    taken(links, load_sem.at[2 * LOADS + 1])
    for part in range(CHUNKS):
        for n in sites(part):
            field[0][n] = forward(coarse_fix, pro[n]).astype(BF16)
        send_wrap(0, part)
    send_rest(0)
    pl.semaphore_wait(met.at[0], 2 + jnp.where(jnp.logical_or(low, high), 1, 2))
    for step in ({"y": 2}, {"y": 6}, {"z": 2}, {"z": 6}):
        signal(met.at[1], partner(step))
    taken(diag, load_sem.at[2 * LOADS + 2])
    local_terms(0)
    near_terms(0)
    pl.semaphore_wait(met.at[1], 4)
    signal(met.at[2], across)
    for part in range(CHUNKS):
        taken(field_in.at[0, 0, pl.ds(0, 2 * SPAN)], wrap_recv.at[0, part])
        for n in sites(part):
            applied = total[n] + hop_terms(0, 0, n)
            field[1][n] = (src[n].astype(F32) - applied).astype(BF16)
        send_wrap(1, part)

    @pl.when(low)
    def _():
        taken(field_in.at[1, 0], wrap_send)

    send_rest(1)

    local_terms(1)
    pl.semaphore_wait(met.at[2], 1)

    @pl.when(z < EARLY)
    def _():
        signal(met.at[3], partner_at(7, {}))

    near_terms(1)
    cross = jnp.zeros((RHS, DOF), F32)
    energy = jnp.zeros((RHS, DOF), F32)
    for part in range(CHUNKS):
        taken(field_in.at[1, 0, pl.ds(0, 2 * SPAN)], wrap_recv.at[1, part])
        for n in sites(part):
            value = total[n] + hop_terms(1, 0, n)
            image[n] = value
            cross += value * field[1][n].astype(F32)
            energy += value * value

    row = lax.broadcasted_iota(jnp.int32, (RHS, DOF), 0)
    lane = lax.broadcasted_iota(jnp.int32, (RHS, DOF), 1)
    cross_at = jnp.sum(cross, axis=1, keepdims=True)
    energy_at = jnp.sum(energy, axis=1, keepdims=True)
    laid = jnp.where(lane == row, cross_at, jnp.where(lane == row + RHS, energy_at, 0.0))
    sums = jnp.sum(laid, axis=0, keepdims=True)

    own = sum_out.at[0]
    sum_out[0] = sums

    def own_copy(slot, depth, step):
        return remote(
            own, direct_in.at[slot], direct_send, direct_recv, partner_at(depth, step)
        )

    @pl.when(high)
    def _():
        pl.semaphore_wait(met.at[3], EARLY)
        for depth in range(EARLY):

            def spread(turned, carry):
                along = lax.rem(turned + 4, 8)
                for slot, step in enumerate(PLANE):
                    own_copy(along * len(PLANE) + slot, depth, {**step, "y": along}).start()
                return carry

            lax.fori_loop(0, 8, spread, 0)

    def along_copy(slot):
        return remote(
            own, sum_in.at[slot], sum_send, sum_recv.at[0], partner({"z": slot + 1})
        )

    @pl.when(jnp.logical_not(high))
    def _():
        for slot in range(EARLY):
            along_copy(slot).start()

    for slot in range(EARLY, 7):
        along_copy(slot).start()

    @pl.when(z < EARLY)
    def _():
        taken(sum_in.at[pl.ds(0, 6)], sum_recv.at[0])

    @pl.when(z >= EARLY)
    def _():
        taken(sum_in.at[pl.ds(0, 7)], sum_recv.at[0])

    for slot in range(7):
        sums = sums + sum_in[slot]

    sum_out[1] = sums
    plane_copies = [
        remote(sum_out.at[1], sum_in.at[7 + slot], sum_send, sum_recv.at[1], partner(step))
        for slot, step in enumerate(offsets_of(("core", "x", "y")))
    ]
    for copy in plane_copies:
        copy.start()
    taken(sum_in.at[pl.ds(7, 63)], sum_recv.at[1])
    sums = sums + jnp.sum(sum_in[7:], axis=0)

    @pl.when(low)
    def _():
        taken(back.at[0, 0, pl.ds(0, 7)], coarse_send)

    @pl.when(jnp.logical_not(low))
    def _():
        taken(back.at[0, 0, pl.ds(0, 6)], coarse_send)

    @pl.when(jnp.logical_not(low))
    def _():
        taken(field_in.at[1, 0], wrap_send)

    taken(links.at[pl.ds(0, 3), pl.ds(0, 11)], field_send)

    @pl.when(high)
    def _():
        taken(sum_in.at[pl.ds(0, 70 - EARLY)], sum_send)
        taken(total.at[pl.ds(0, 2 * EARLY)], direct_send)

    @pl.when(jnp.logical_not(high))
    def _():
        taken(sum_in, sum_send)

    @pl.when(z < EARLY)
    def _():
        taken(direct_in, direct_recv)

    sums = sums + jnp.sum(direct_in[...], axis=0)

    wide = jnp.broadcast_to(sums, (RHS, DOF))
    cross_sum = jnp.sum(jnp.where(lane == row, wide, 0.0), axis=1, keepdims=True)
    energy_sum = jnp.sum(jnp.where(lane == row + RHS, wide, 0.0), axis=1, keepdims=True)
    factor[...] = jnp.broadcast_to(cross_sum / (energy_sum + 1e-06), (RHS, DOF))


def body(source, diag_block, link_time, link_zaxis, link_yaxis, link_xaxis, prolong,
         top_diag, top_time, top_zaxis, top_yaxis):
    shape = source.shape
    blocks = [
        value.reshape(NX, DOF, DOF)
        for value in (diag_block, link_time, link_zaxis, link_yaxis, link_xaxis, prolong)
    ]
    tops = [value.reshape(DOF, DOF) for value in (top_diag, top_time, top_zaxis, top_yaxis)]
    vmem, dma = pltpu.VMEM, pltpu.SemaphoreType.DMA
    total = 7 + 63
    lifted, resid, image, factor = pl.pallas_call(
        kernel,
        out_shape=(
            vmem((NX, RHS, DOF), BF16),
            vmem((NX, RHS, DOF), BF16),
            vmem((NX, RHS, DOF), F32),
            vmem((RHS, DOF), F32),
        ),
        in_specs=[pl.BlockSpec(memory_space=pltpu.HBM)] * 11,
        out_specs=[pl.BlockSpec(memory_space=pltpu.VMEM)] * 4,
        scratch_shapes=[
            vmem((NX, RHS, DOF), BF16),
            vmem((NX, DOF, DOF), BF16),
            vmem((4, NX, DOF, DOF), BF16),
            vmem((NX, DOF, DOF), BF16),
            vmem((4, DOF, DOF), BF16),
            vmem((2, 3, NX, RHS, DOF), BF16),
            vmem((2, 3, NX, RHS, DOF), BF16),
            vmem((2, 3, NX, RHS, DOF), BF16),
            vmem((NX, RHS, DOF), F32),
            vmem((4, RHS, DOF), BF16),
            vmem((3, RHS, DOF), BF16),
            vmem((3, RHS, DOF), BF16),
            vmem((2, 1, DOF), F32),
            vmem((total, 1, DOF), F32),
            vmem((64, 1, DOF), F32),
            dma((2 * LOADS + 3,)),
            dma,
            dma((2,)),
            dma,
            dma,
            dma((2, 2)),
            dma((2, CHUNKS)),
            dma,
            dma((2,)),
            dma,
            dma,
            vmem((RHS, DOF), BF16),
            dma,
            pltpu.SemaphoreType.REGULAR,
            pltpu.SemaphoreType.REGULAR((4,)),
        ],
        compiler_params=pltpu.CompilerParams(
            collective_id=0, has_side_effects=True, vmem_limit_bytes=60 * 1024 * 1024
        ),
        name="smooth",
    )(source.reshape(NX, RHS, DOF), *blocks, *tops)
    wide = resid.astype(F32)
    update = lifted.astype(F32) + factor * wide
    remainder = wide - factor * image
    return update.reshape(shape), remainder.reshape(shape)


def solution(mesh):
    field = P("ta", "gz", "yx", None, None, None)
    top = P("ta", "gz", "yx", None, None)
    return jax.shard_map(
        body, mesh=mesh, in_specs=(field,) * 7 + (top,) * 4, out_specs=(field, field), check_vma=False
    )
```

```python
import itertools

import jax
import jax.numpy as jnp
from jax import lax
from jax.experimental import pallas as pl
from jax.experimental.pallas import tpu as pltpu
from jax.sharding import PartitionSpec as P

MESH = pl.DeviceIdType.MESH
F32 = jnp.float32
BF16 = jnp.bfloat16

NX, RHS, DOF = 12, 32, 128
CHUNKS = 2
LOADS = 2
SPAN = NX // CHUNKS
SIZES = {"core": 2, "x": 4, "y": 8, "z": 8}
EARLY = 4


def offsets_of(axes):
    every = itertools.product(*(range(SIZES[axis]) for axis in axes))
    return [dict(zip(axes, step)) for step in every if any(step)]


PLANE = [{}] + offsets_of(("core", "x"))


def forward(vector, block):
    return lax.dot_general(vector, block, (((1,), (1,)), ((), ())), preferred_element_type=F32)


def adjoint(vector, block):
    return lax.dot_general(vector, block, (((1,), (0,)), ((), ())), preferred_element_type=F32)


def halves(value):
    high = value.astype(BF16)
    low = (value - high.astype(F32)).astype(BF16)
    return jnp.concatenate([high, low], axis=0)


def fold(value):
    return value[:RHS] + value[RHS:]


def kernel(
    src_h, diag_h, lt_h, lz_h, ly_h, lx_h, pro_h, td_h, tt_h, tz_h, ty_h,
    lifted, resid, image, factor,
    src, diag, links, pro, tops,
    back, field_in, back_in, total,
    coarse, coarse_in, hop_in,
    sum_out, sum_in, direct_in,
    load_sem, coarse_send, coarse_recv, field_send, wrap_send, near_recv, wrap_recv,
    sum_send, sum_recv, direct_send, direct_recv,
    relay_in, relay_recv, late_in, met,
):
    field = (lifted, resid)
    ta, gz, yx = lax.axis_index("ta"), lax.axis_index("gz"), lax.axis_index("yx")

    def at(ta_at, gz_at, yx_at):
        return (ta_at, gz_at, yx_at)

    plus = (
        at(lax.rem(ta + 1, 16), gz, yx),
        at(ta, lax.rem(gz + 1, 8), yx),
        at(ta, gz, lax.rem(yx + 1, 4)),
    )
    minus = (
        at(lax.rem(ta + 15, 16), gz, yx),
        at(ta, lax.rem(gz + 7, 8), yx),
        at(ta, gz, lax.rem(yx + 3, 4)),
    )
    here = {
        "core": lax.rem(gz, 2),
        "x": yx,
        "y": (ta // 8) * 4 + gz // 2,
        "z": lax.rem(ta, 8),
    }

    def partner(step):
        place = {
            axis: lax.rem(here[axis] + step[axis], size) if axis in step else here[axis]
            for axis, size in SIZES.items()
        }
        return at(
            (place["y"] // 4) * 8 + place["z"],
            lax.rem(place["y"], 4) * 2 + place["core"],
            place["x"],
        )

    y, z = here["y"], here["z"]
    low, high = z == 0, z == 7
    across = partner({"y": 4})
    below, above = partner({"z": 7}), partner({"z": 1})

    direct_in[...] = jnp.zeros_like(direct_in)
    for slot in range(EARLY):
        sum_in[slot] = jnp.zeros((1, DOF), F32)

    def partner_at(depth, step):
        ta_at, gz_at, yx_at = partner(step)
        return at((ta_at // 8) * 8 + depth, gz_at, yx_at)

    def taken(ref, semaphore):
        pltpu.make_async_copy(ref, ref, semaphore).wait()

    def load(source, target, slot):
        pltpu.make_async_copy(source, target, load_sem.at[slot]).start()

    for part in range(LOADS):
        some = pl.ds(part * (NX // LOADS), NX // LOADS)
        load(pro_h.at[some], pro.at[some], 2 * part)
        load(src_h.at[some], src.at[some], 2 * part + 1)
    for slot, source in enumerate((tt_h, tz_h, ty_h, td_h)):
        load(source, tops.at[slot], 2 * LOADS)

    def signal(semaphore, device):
        pl.semaphore_signal(semaphore, inc=1, device_id=device, device_id_type=MESH)

    barrier = pltpu.get_barrier_semaphore()
    for device in [plus[1], minus[1], plus[2], minus[2], partner({"y": 1}), partner({"y": 7})]:
        signal(barrier, device)
    for step in offsets_of(("core", "x")):
        signal(barrier, partner(step))

    @pl.when(low)
    def _():
        signal(barrier, minus[0])
        signal(barrier, below)
        signal(barrier, across)

    @pl.when(jnp.logical_not(low))
    def _():
        signal(barrier, minus[0])

    @pl.when(jnp.logical_not(high))
    def _():
        signal(barrier, plus[0])

    greetings = 13 + jnp.where(high, 3, 2)

    def remote(source, target, send, recv, device):
        return pltpu.make_async_remote_copy(
            src_ref=source, dst_ref=target, send_sem=send, recv_sem=recv,
            device_id=device, device_id_type=MESH,
        )

    restricted = jnp.zeros((RHS, DOF), F32)
    for part in range(LOADS):
        some = pl.ds(part * (NX // LOADS), NX // LOADS)
        taken(pro.at[some], load_sem.at[2 * part])
        taken(src.at[some], load_sem.at[2 * part + 1])
        for n in range(part * (NX // LOADS), (part + 1) * (NX // LOADS)):
            restricted += adjoint(src[n], pro[n])
    coarse[0] = restricted
    split = halves(restricted)
    for slot, source in enumerate((lt_h, lz_h, ly_h, lx_h)):
        load(source, links.at[slot], 2 * LOADS + 1)
    load(diag_h, diag, 2 * LOADS + 2)

    taken(tops, load_sem.at[2 * LOADS])
    coarse[1] = fold(adjoint(split, tops[0]))

    pl.semaphore_wait(barrier, greetings)

    def value_copy(mu, device):
        return remote(coarse.at[0], coarse_in.at[mu], coarse_send, coarse_recv.at[min(mu, 1)], device)

    def hop_copy(mu):
        return remote(coarse.at[1 + mu], hop_in.at[mu], coarse_send, coarse_recv.at[min(mu, 1)], plus[mu])

    hop_copy(0).start()
    to_relay = remote(coarse.at[0], relay_in, coarse_send, relay_recv, across)
    from_relay = remote(relay_in, coarse_in.at[0], coarse_send, coarse_recv.at[0], below)

    @pl.when(low)
    def _():
        to_relay.start()

    @pl.when(jnp.logical_not(low))
    def _():
        value_copy(0, minus[0]).start()

    for mu in (1, 2):
        value_copy(mu, minus[mu]).start()

    @pl.when(high)
    def _():
        signal(late_in, above)

    signal(met.at[0], partner({"y": 1}))
    signal(met.at[0], partner({"y": 7}))

    @pl.when(jnp.logical_not(low))
    def _():
        signal(met.at[0], below)

    @pl.when(jnp.logical_not(jnp.logical_or(low, high)))
    def _():
        signal(met.at[0], above)

    for mu in (1, 2):
        coarse[1 + mu] = fold(adjoint(split, tops[mu]))
        hop_copy(mu).start()

    @pl.when(low)
    def _():
        to_relay.wait_recv()
        pl.semaphore_wait(late_in, 1)
        from_relay.start()
        signal(met.at[0], above)

    correction = fold(forward(split, tops[3]))
    taken(total.at[pl.ds(0, 4)], coarse_recv.at[1])
    for mu in (2, 1):
        correction += fold(forward(halves(coarse_in[mu]), tops[mu])) + hop_in[mu]
    taken(total.at[pl.ds(0, 2)], coarse_recv.at[0])
    correction += fold(forward(halves(coarse_in[0]), tops[0])) + hop_in[0]
    coarse_fix = correction.astype(BF16)

    def span(part):
        return pl.ds(part * SPAN, SPAN)

    def landing(turn, mu, part):
        return near_recv.at[turn, mu - 1] if mu else wrap_recv.at[turn, part]

    def field_copy(turn, mu, part):
        return remote(
            field[turn].at[span(part)], field_in.at[turn, mu, span(part)],
            wrap_send if (turn, mu) == (1, 0) else field_send, landing(turn, mu, part), minus[mu],
        )

    def back_copy(turn, mu, part):
        return remote(
            back.at[turn, mu, span(part)], back_in.at[turn, mu, span(part)],
            field_send, landing(turn, mu, part), plus[mu],
        )

    def sites(part):
        return range(part * SPAN, (part + 1) * SPAN)

    def send_back(turn, mu, part):
        for n in sites(part):
            back[turn, mu, n] = adjoint(field[turn][n], links[mu, n]).astype(BF16)
        back_copy(turn, mu, part).start()

    def local_terms(turn):
        for n in range(NX):
            after, before = (n + 1) % NX, (n - 1) % NX
            value = forward(field[turn][n], diag[n])
            value += forward(field[turn][after], links[3, n])
            value += adjoint(field[turn][before], links[3, before]).astype(BF16).astype(F32)
            total[n] = value

    def hop_terms(turn, mu, n):
        return forward(field_in[turn, mu, n], links[mu, n]) + back_in[turn, mu, n].astype(F32)

    def near_terms(turn):
        for mu in (2, 1):
            taken(field_in.at[turn, pl.ds(0, 2)], near_recv.at[turn, mu - 1])
            for n in range(NX):
                total[n] += hop_terms(turn, mu, n)

    def send_wrap(turn, part):
        @pl.when(low)
        def _():
            field_copy(turn, 0, part).start()

        for n in sites(part):
            back[turn, 0, n] = adjoint(field[turn][n], links[0, n]).astype(BF16)

        @pl.when(high)
        def _():
            back_copy(turn, 0, part).start()

    def send_rest(turn):
        for mu in (2, 1):
            for part in range(CHUNKS):
                field_copy(turn, mu, part).start()
        for mu in (2, 1):
            for part in range(CHUNKS):
                send_back(turn, mu, part)
        for part in range(CHUNKS):

            @pl.when(jnp.logical_not(low))
            def _():
                field_copy(turn, 0, part).start()

            @pl.when(jnp.logical_not(high))
            def _():
                back_copy(turn, 0, part).start()

    taken(links, load_sem.at[2 * LOADS + 1])
    for part in range(CHUNKS):
        for n in sites(part):
            field[0][n] = forward(coarse_fix, pro[n]).astype(BF16)
        send_wrap(0, part)
    send_rest(0)
    pl.semaphore_wait(met.at[0], 2 + jnp.where(jnp.logical_or(low, high), 1, 2))
    for step in ({"y": 2}, {"y": 6}, {"z": 2}, {"z": 6}):
        signal(met.at[1], partner(step))
    taken(diag, load_sem.at[2 * LOADS + 2])
    local_terms(0)
    near_terms(0)
    pl.semaphore_wait(met.at[1], 4)
    signal(met.at[2], across)
    for part in range(CHUNKS):
        taken(field_in.at[0, 0, pl.ds(0, 2 * SPAN)], wrap_recv.at[0, part])
        for n in sites(part):
            applied = total[n] + hop_terms(0, 0, n)
            field[1][n] = (src[n].astype(F32) - applied).astype(BF16)
        send_wrap(1, part)

    @pl.when(low)
    def _():
        taken(field_in.at[1, 0], wrap_send)

    send_rest(1)

    local_terms(1)
    pl.semaphore_wait(met.at[2], 1)

    @pl.when(z < EARLY)
    def _():
        signal(met.at[3], partner_at(7, {}))

    near_terms(1)
    cross = jnp.zeros((RHS, DOF), F32)
    energy = jnp.zeros((RHS, DOF), F32)
    for part in range(CHUNKS):
        taken(field_in.at[1, 0, pl.ds(0, 2 * SPAN)], wrap_recv.at[1, part])
        for n in sites(part):
            value = total[n] + hop_terms(1, 0, n)
            image[n] = value
            cross += value * field[1][n].astype(F32)
            energy += value * value

    row = lax.broadcasted_iota(jnp.int32, (RHS, DOF), 0)
    lane = lax.broadcasted_iota(jnp.int32, (RHS, DOF), 1)
    cross_at = jnp.sum(cross, axis=1, keepdims=True)
    energy_at = jnp.sum(energy, axis=1, keepdims=True)
    laid = jnp.where(lane == row, cross_at, jnp.where(lane == row + RHS, energy_at, 0.0))
    sums = jnp.sum(laid, axis=0, keepdims=True)

    own = sum_out.at[0]
    sum_out[0] = sums

    def own_copy(slot, depth, step):
        return remote(
            own, direct_in.at[slot], direct_send, direct_recv, partner_at(depth, step)
        )

    @pl.when(high)
    def _():
        pl.semaphore_wait(met.at[3], EARLY)
        for depth in range(EARLY):

            def spread(turned, carry):
                along = lax.rem(turned + 4, 8)
                for slot, step in enumerate(PLANE):
                    own_copy(along * len(PLANE) + slot, depth, {**step, "y": along}).start()
                return carry

            lax.fori_loop(0, 8, spread, 0)

    def along_copy(slot):
        return remote(
            own, sum_in.at[slot], sum_send, sum_recv.at[0], partner({"z": slot + 1})
        )

    @pl.when(jnp.logical_not(high))
    def _():
        for slot in range(EARLY):
            along_copy(slot).start()

    for slot in range(EARLY, 7):
        along_copy(slot).start()

    @pl.when(z < EARLY)
    def _():
        taken(sum_in.at[pl.ds(0, 6)], sum_recv.at[0])

    @pl.when(z >= EARLY)
    def _():
        taken(sum_in.at[pl.ds(0, 7)], sum_recv.at[0])

    for slot in range(7):
        sums = sums + sum_in[slot]

    sum_out[1] = sums
    plane_copies = [
        remote(sum_out.at[1], sum_in.at[7 + slot], sum_send, sum_recv.at[1], partner(step))
        for slot, step in enumerate(offsets_of(("core", "x", "y")))
    ]
    for copy in plane_copies:
        copy.start()
    taken(sum_in.at[pl.ds(7, 63)], sum_recv.at[1])
    sums = sums + jnp.sum(sum_in[7:], axis=0)

    @pl.when(low)
    def _():
        taken(total.at[pl.ds(0, 7)], coarse_send)

    @pl.when(jnp.logical_not(low))
    def _():
        taken(total.at[pl.ds(0, 6)], coarse_send)

    @pl.when(jnp.logical_not(low))
    def _():
        taken(field_in.at[1, 0], wrap_send)

    taken(links.at[pl.ds(0, 3), pl.ds(0, 11)], field_send)

    @pl.when(high)
    def _():
        taken(sum_in.at[pl.ds(0, 70 - EARLY)], sum_send)
        taken(total.at[pl.ds(0, 2 * EARLY)], direct_send)

    @pl.when(jnp.logical_not(high))
    def _():
        taken(sum_in, sum_send)

    @pl.when(z < EARLY)
    def _():
        taken(direct_in, direct_recv)

    sums = sums + jnp.sum(direct_in[...], axis=0)

    wide = jnp.broadcast_to(sums, (RHS, DOF))
    cross_sum = jnp.sum(jnp.where(lane == row, wide, 0.0), axis=1, keepdims=True)
    energy_sum = jnp.sum(jnp.where(lane == row + RHS, wide, 0.0), axis=1, keepdims=True)
    factor[...] = jnp.broadcast_to(cross_sum / (energy_sum + 1e-06), (RHS, DOF))


def body(source, diag_block, link_time, link_zaxis, link_yaxis, link_xaxis, prolong,
         top_diag, top_time, top_zaxis, top_yaxis):
    shape = source.shape
    blocks = [
        value.reshape(NX, DOF, DOF)
        for value in (diag_block, link_time, link_zaxis, link_yaxis, link_xaxis, prolong)
    ]
    tops = [value.reshape(DOF, DOF) for value in (top_diag, top_time, top_zaxis, top_yaxis)]
    vmem, dma = pltpu.VMEM, pltpu.SemaphoreType.DMA
    total = 7 + 63
    lifted, resid, image, factor = pl.pallas_call(
        kernel,
        out_shape=(
            vmem((NX, RHS, DOF), BF16),
            vmem((NX, RHS, DOF), BF16),
            vmem((NX, RHS, DOF), F32),
            vmem((RHS, DOF), F32),
        ),
        in_specs=[pl.BlockSpec(memory_space=pltpu.HBM)] * 11,
        out_specs=[pl.BlockSpec(memory_space=pltpu.VMEM)] * 4,
        scratch_shapes=[
            vmem((NX, RHS, DOF), BF16),
            vmem((NX, DOF, DOF), BF16),
            vmem((4, NX, DOF, DOF), BF16),
            vmem((NX, DOF, DOF), BF16),
            vmem((4, DOF, DOF), BF16),
            vmem((2, 3, NX, RHS, DOF), BF16),
            vmem((2, 3, NX, RHS, DOF), BF16),
            vmem((2, 3, NX, RHS, DOF), BF16),
            vmem((NX, RHS, DOF), F32),
            vmem((4, RHS, DOF), F32),
            vmem((3, RHS, DOF), F32),
            vmem((3, RHS, DOF), F32),
            vmem((2, 1, DOF), F32),
            vmem((total, 1, DOF), F32),
            vmem((64, 1, DOF), F32),
            dma((2 * LOADS + 3,)),
            dma,
            dma((2,)),
            dma,
            dma,
            dma((2, 2)),
            dma((2, CHUNKS)),
            dma,
            dma((2,)),
            dma,
            dma,
            vmem((RHS, DOF), F32),
            dma,
            pltpu.SemaphoreType.REGULAR,
            pltpu.SemaphoreType.REGULAR((4,)),
        ],
        compiler_params=pltpu.CompilerParams(
            collective_id=0, has_side_effects=True, vmem_limit_bytes=60 * 1024 * 1024
        ),
        name="smooth",
    )(source.reshape(NX, RHS, DOF), *blocks, *tops)
    wide = resid.astype(F32)
    update = lifted.astype(F32) + factor * wide
    remainder = wide - factor * image
    return update.reshape(shape), remainder.reshape(shape)


def solution(mesh):
    field = P("ta", "gz", "yx", None, None, None)
    top = P("ta", "gz", "yx", None, None)
    return jax.shard_map(
        body, mesh=mesh, in_specs=(field,) * 7 + (top,) * 4, out_specs=(field, field), check_vma=False
    )
```

```python
import itertools

import jax
import jax.numpy as jnp
from jax import lax
from jax.experimental import pallas as pl
from jax.experimental.pallas import tpu as pltpu
from jax.sharding import PartitionSpec as P

MESH = pl.DeviceIdType.MESH
F32 = jnp.float32
BF16 = jnp.bfloat16

NX, RHS, DOF = 12, 32, 128
CHUNKS = 2
LOADS = 2
SPAN = NX // CHUNKS
SIZES = {"core": 2, "x": 4, "y": 8, "z": 8}
EARLY = 4


def offsets_of(axes):
    every = itertools.product(*(range(SIZES[axis]) for axis in axes))
    return [dict(zip(axes, step)) for step in every if any(step)]


PLANE = [{}] + offsets_of(("core", "x"))


def forward(vector, block):
    return lax.dot_general(vector, block, (((1,), (1,)), ((), ())), preferred_element_type=F32)


def adjoint(vector, block):
    return lax.dot_general(vector, block, (((1,), (0,)), ((), ())), preferred_element_type=F32)


def halves(value):
    high = value.astype(BF16)
    low = (value - high.astype(F32)).astype(BF16)
    return jnp.concatenate([high, low], axis=0)


def fold(value):
    return value[:RHS] + value[RHS:]


def kernel(
    src_h, diag_h, lt_h, lz_h, ly_h, lx_h, pro_h, td_h, tt_h, tz_h, ty_h,
    lifted, resid, image, factor,
    src, diag, links, pro, tops,
    back, field_in, back_in, total,
    coarse, coarse_in, hop_in,
    sum_out, sum_in, direct_in,
    load_sem, coarse_send, coarse_recv, field_send, wrap_send, near_recv, wrap_recv,
    sum_send, sum_recv, direct_send, direct_recv,
    relay_in, relay_recv, late_in, met,
):
    field = (lifted, resid)
    ta, gz, yx = lax.axis_index("ta"), lax.axis_index("gz"), lax.axis_index("yx")

    def at(ta_at, gz_at, yx_at):
        return (ta_at, gz_at, yx_at)

    plus = (
        at(lax.rem(ta + 1, 16), gz, yx),
        at(ta, lax.rem(gz + 1, 8), yx),
        at(ta, gz, lax.rem(yx + 1, 4)),
    )
    minus = (
        at(lax.rem(ta + 15, 16), gz, yx),
        at(ta, lax.rem(gz + 7, 8), yx),
        at(ta, gz, lax.rem(yx + 3, 4)),
    )
    here = {
        "core": lax.rem(gz, 2),
        "x": yx,
        "y": (ta // 8) * 4 + gz // 2,
        "z": lax.rem(ta, 8),
    }

    def partner(step):
        place = {
            axis: lax.rem(here[axis] + step[axis], size) if axis in step else here[axis]
            for axis, size in SIZES.items()
        }
        return at(
            (place["y"] // 4) * 8 + place["z"],
            lax.rem(place["y"], 4) * 2 + place["core"],
            place["x"],
        )

    y, z = here["y"], here["z"]
    low, high = z == 0, z == 7
    across = partner({"y": 4})
    below, above = partner({"z": 7}), partner({"z": 1})

    def partner_at(depth, step):
        ta_at, gz_at, yx_at = partner(step)
        return at((ta_at // 8) * 8 + depth, gz_at, yx_at)

    def taken(ref, semaphore):
        pltpu.make_async_copy(ref, ref, semaphore).wait()

    def load(source, target, slot):
        pltpu.make_async_copy(source, target, load_sem.at[slot]).start()

    for part in range(LOADS):
        some = pl.ds(part * (NX // LOADS), NX // LOADS)
        load(pro_h.at[some], pro.at[some], 2 * part)
        load(src_h.at[some], src.at[some], 2 * part + 1)
    for slot, source in enumerate((tt_h, tz_h, ty_h, td_h)):
        load(source, tops.at[slot], 2 * LOADS)

    direct_in[...] = jnp.zeros_like(direct_in)
    for slot in range(EARLY):
        sum_in[slot] = jnp.zeros((1, DOF), F32)

    def signal(semaphore, device):
        pl.semaphore_signal(semaphore, inc=1, device_id=device, device_id_type=MESH)

    barrier = pltpu.get_barrier_semaphore()
    for device in [plus[1], minus[1], plus[2], minus[2], partner({"y": 1}), partner({"y": 7})]:
        signal(barrier, device)
    for step in offsets_of(("core", "x")):
        signal(barrier, partner(step))

    @pl.when(low)
    def _():
        signal(barrier, minus[0])
        signal(barrier, below)
        signal(barrier, across)

    @pl.when(jnp.logical_not(low))
    def _():
        signal(barrier, minus[0])

    @pl.when(jnp.logical_not(high))
    def _():
        signal(barrier, plus[0])

    greetings = 13 + jnp.where(high, 3, 2)

    def remote(source, target, send, recv, device):
        return pltpu.make_async_remote_copy(
            src_ref=source, dst_ref=target, send_sem=send, recv_sem=recv,
            device_id=device, device_id_type=MESH,
        )

    restricted = jnp.zeros((RHS, DOF), F32)
    for part in range(LOADS):
        some = pl.ds(part * (NX // LOADS), NX // LOADS)
        taken(pro.at[some], load_sem.at[2 * part])
        taken(src.at[some], load_sem.at[2 * part + 1])
        for n in range(part * (NX // LOADS), (part + 1) * (NX // LOADS)):
            restricted += adjoint(src[n], pro[n])
    coarse[0] = restricted
    split = halves(restricted)
    for slot, source in enumerate((lt_h, lz_h, ly_h, lx_h)):
        load(source, links.at[slot], 2 * LOADS + 1)
    load(diag_h, diag, 2 * LOADS + 2)

    taken(tops, load_sem.at[2 * LOADS])
    coarse[1] = fold(adjoint(split, tops[0]))

    pl.semaphore_wait(barrier, greetings)

    def value_copy(mu, device):
        return remote(coarse.at[0], coarse_in.at[mu], coarse_send, coarse_recv.at[min(mu, 1)], device)

    def hop_copy(mu):
        return remote(coarse.at[1 + mu], hop_in.at[mu], coarse_send, coarse_recv.at[min(mu, 1)], plus[mu])

    hop_copy(0).start()
    to_relay = remote(coarse.at[0], relay_in, coarse_send, relay_recv, across)
    from_relay = remote(relay_in, coarse_in.at[0], coarse_send, coarse_recv.at[0], below)

    @pl.when(low)
    def _():
        to_relay.start()

    @pl.when(jnp.logical_not(low))
    def _():
        value_copy(0, minus[0]).start()

    for mu in (1, 2):
        value_copy(mu, minus[mu]).start()

    @pl.when(high)
    def _():
        signal(late_in, above)

    signal(met.at[0], partner({"y": 1}))
    signal(met.at[0], partner({"y": 7}))

    @pl.when(jnp.logical_not(low))
    def _():
        signal(met.at[0], below)

    @pl.when(jnp.logical_not(jnp.logical_or(low, high)))
    def _():
        signal(met.at[0], above)

    for mu in (1, 2):
        coarse[1 + mu] = fold(adjoint(split, tops[mu]))
        hop_copy(mu).start()

    @pl.when(low)
    def _():
        to_relay.wait_recv()
        pl.semaphore_wait(late_in, 1)
        from_relay.start()
        signal(met.at[0], above)

    correction = fold(forward(split, tops[3]))
    taken(total.at[pl.ds(0, 4)], coarse_recv.at[1])
    for mu in (2, 1):
        correction += fold(forward(halves(coarse_in[mu]), tops[mu])) + hop_in[mu]
    taken(total.at[pl.ds(0, 2)], coarse_recv.at[0])
    correction += fold(forward(halves(coarse_in[0]), tops[0])) + hop_in[0]
    coarse_fix = correction.astype(BF16)

    def span(part):
        return pl.ds(part * SPAN, SPAN)

    def landing(turn, mu, part):
        return near_recv.at[turn, mu - 1] if mu else wrap_recv.at[turn, part]

    def field_copy(turn, mu, part):
        return remote(
            field[turn].at[span(part)], field_in.at[turn, mu, span(part)],
            wrap_send if (turn, mu) == (1, 0) else field_send, landing(turn, mu, part), minus[mu],
        )

    def back_copy(turn, mu, part):
        return remote(
            back.at[turn, mu, span(part)], back_in.at[turn, mu, span(part)],
            field_send, landing(turn, mu, part), plus[mu],
        )

    def sites(part):
        return range(part * SPAN, (part + 1) * SPAN)

    def send_back(turn, mu, part):
        for n in sites(part):
            back[turn, mu, n] = adjoint(field[turn][n], links[mu, n]).astype(BF16)
        back_copy(turn, mu, part).start()

    def local_terms(turn):
        for n in range(NX):
            after, before = (n + 1) % NX, (n - 1) % NX
            value = forward(field[turn][n], diag[n])
            value += forward(field[turn][after], links[3, n])
            value += adjoint(field[turn][before], links[3, before]).astype(BF16).astype(F32)
            total[n] = value

    def hop_terms(turn, mu, n):
        return forward(field_in[turn, mu, n], links[mu, n]) + back_in[turn, mu, n].astype(F32)

    def near_terms(turn):
        for mu in (2, 1):
            taken(field_in.at[turn, pl.ds(0, 2)], near_recv.at[turn, mu - 1])
            for n in range(NX):
                total[n] += hop_terms(turn, mu, n)

    def send_wrap(turn, part):
        if turn:

            @pl.when(low)
            def _():
                field_copy(turn, 0, part).start()

        for n in sites(part):
            back[turn, 0, n] = adjoint(field[turn][n], links[0, n]).astype(BF16)

        @pl.when(high)
        def _():
            back_copy(turn, 0, part).start()

    def send_rest(turn):
        for mu in (2, 1):
            for part in range(CHUNKS):
                field_copy(turn, mu, part).start()
        for mu in (2, 1):
            for part in range(CHUNKS):
                send_back(turn, mu, part)
        for part in range(CHUNKS):

            @pl.when(jnp.logical_not(low))
            def _():
                field_copy(turn, 0, part).start()

            @pl.when(jnp.logical_not(high))
            def _():
                back_copy(turn, 0, part).start()

    taken(links, load_sem.at[2 * LOADS + 1])
    for part in range(CHUNKS):
        for n in sites(part):
            field[0][n] = forward(coarse_fix, pro[n]).astype(BF16)

        @pl.when(low)
        def _():
            field_copy(0, 0, part).start()

    for part in range(CHUNKS):
        send_wrap(0, part)
    send_rest(0)
    pl.semaphore_wait(met.at[0], 2 + jnp.where(jnp.logical_or(low, high), 1, 2))
    for step in ({"y": 2}, {"y": 6}, {"z": 2}, {"z": 6}):
        signal(met.at[1], partner(step))
    taken(diag, load_sem.at[2 * LOADS + 2])
    local_terms(0)
    near_terms(0)
    pl.semaphore_wait(met.at[1], 4)
    signal(met.at[2], across)
    for part in range(CHUNKS):
        taken(field_in.at[0, 0, pl.ds(0, 2 * SPAN)], wrap_recv.at[0, part])
        for n in sites(part):
            applied = total[n] + hop_terms(0, 0, n)
            field[1][n] = (src[n].astype(F32) - applied).astype(BF16)
        send_wrap(1, part)

    @pl.when(low)
    def _():
        taken(field_in.at[1, 0], wrap_send)

    send_rest(1)

    local_terms(1)
    pl.semaphore_wait(met.at[2], 1)

    @pl.when(z < EARLY)
    def _():
        signal(met.at[3], partner_at(7, {}))

    near_terms(1)
    cross = jnp.zeros((RHS, DOF), F32)
    energy = jnp.zeros((RHS, DOF), F32)
    for part in range(CHUNKS):
        taken(field_in.at[1, 0, pl.ds(0, 2 * SPAN)], wrap_recv.at[1, part])
        for n in sites(part):
            value = total[n] + hop_terms(1, 0, n)
            image[n] = value
            cross += value * field[1][n].astype(F32)
            energy += value * value

    row = lax.broadcasted_iota(jnp.int32, (RHS, DOF), 0)
    lane = lax.broadcasted_iota(jnp.int32, (RHS, DOF), 1)
    cross_at = jnp.sum(cross, axis=1, keepdims=True)
    energy_at = jnp.sum(energy, axis=1, keepdims=True)
    laid = jnp.where(lane == row, cross_at, jnp.where(lane == row + RHS, energy_at, 0.0))
    sums = jnp.sum(laid, axis=0, keepdims=True)

    own = sum_out.at[0]
    sum_out[0] = sums

    def own_copy(slot, depth, step):
        return remote(
            own, direct_in.at[slot], direct_send, direct_recv, partner_at(depth, step)
        )

    @pl.when(high)
    def _():
        pl.semaphore_wait(met.at[3], EARLY)
        for depth in range(EARLY):

            def spread(turned, carry):
                along = lax.rem(turned + 4, 8)
                for slot, step in enumerate(PLANE):
                    own_copy(along * len(PLANE) + slot, depth, {**step, "y": along}).start()
                return carry

            lax.fori_loop(0, 8, spread, 0)

    def along_copy(slot):
        return remote(
            own, sum_in.at[slot], sum_send, sum_recv.at[0], partner({"z": slot + 1})
        )

    @pl.when(jnp.logical_not(high))
    def _():
        for slot in range(EARLY):
            along_copy(slot).start()

    for slot in range(EARLY, 7):
        along_copy(slot).start()

    @pl.when(z < EARLY)
    def _():
        taken(sum_in.at[pl.ds(0, 6)], sum_recv.at[0])

    @pl.when(z >= EARLY)
    def _():
        taken(sum_in.at[pl.ds(0, 7)], sum_recv.at[0])

    for slot in range(7):
        sums = sums + sum_in[slot]

    sum_out[1] = sums
    plane_copies = [
        remote(sum_out.at[1], sum_in.at[7 + slot], sum_send, sum_recv.at[1], partner(step))
        for slot, step in enumerate(offsets_of(("core", "x", "y")))
    ]
    for copy in plane_copies:
        copy.start()
    taken(sum_in.at[pl.ds(7, 63)], sum_recv.at[1])
    sums = sums + jnp.sum(sum_in[7:], axis=0)

    @pl.when(low)
    def _():
        taken(total.at[pl.ds(0, 7)], coarse_send)

    @pl.when(jnp.logical_not(low))
    def _():
        taken(total.at[pl.ds(0, 6)], coarse_send)

    @pl.when(jnp.logical_not(low))
    def _():
        taken(field_in.at[1, 0], wrap_send)

    taken(links.at[pl.ds(0, 3), pl.ds(0, 11)], field_send)

    @pl.when(high)
    def _():
        taken(sum_in.at[pl.ds(0, 70 - EARLY)], sum_send)
        taken(total.at[pl.ds(0, 2 * EARLY)], direct_send)

    @pl.when(jnp.logical_not(high))
    def _():
        taken(sum_in, sum_send)

    @pl.when(z < EARLY)
    def _():
        taken(direct_in, direct_recv)

    sums = sums + jnp.sum(direct_in[...], axis=0)

    wide = jnp.broadcast_to(sums, (RHS, DOF))
    cross_sum = jnp.sum(jnp.where(lane == row, wide, 0.0), axis=1, keepdims=True)
    energy_sum = jnp.sum(jnp.where(lane == row + RHS, wide, 0.0), axis=1, keepdims=True)
    factor[...] = jnp.broadcast_to(cross_sum / (energy_sum + 1e-06), (RHS, DOF))


def body(source, diag_block, link_time, link_zaxis, link_yaxis, link_xaxis, prolong,
         top_diag, top_time, top_zaxis, top_yaxis):
    shape = source.shape
    blocks = [
        value.reshape(NX, DOF, DOF)
        for value in (diag_block, link_time, link_zaxis, link_yaxis, link_xaxis, prolong)
    ]
    tops = [value.reshape(DOF, DOF) for value in (top_diag, top_time, top_zaxis, top_yaxis)]
    vmem, dma = pltpu.VMEM, pltpu.SemaphoreType.DMA
    total = 7 + 63
    lifted, resid, image, factor = pl.pallas_call(
        kernel,
        out_shape=(
            vmem((NX, RHS, DOF), BF16),
            vmem((NX, RHS, DOF), BF16),
            vmem((NX, RHS, DOF), F32),
            vmem((RHS, DOF), F32),
        ),
        in_specs=[pl.BlockSpec(memory_space=pltpu.HBM)] * 11,
        out_specs=[pl.BlockSpec(memory_space=pltpu.VMEM)] * 4,
        scratch_shapes=[
            vmem((NX, RHS, DOF), BF16),
            vmem((NX, DOF, DOF), BF16),
            vmem((4, NX, DOF, DOF), BF16),
            vmem((NX, DOF, DOF), BF16),
            vmem((4, DOF, DOF), BF16),
            vmem((2, 3, NX, RHS, DOF), BF16),
            vmem((2, 3, NX, RHS, DOF), BF16),
            vmem((2, 3, NX, RHS, DOF), BF16),
            vmem((NX, RHS, DOF), F32),
            vmem((4, RHS, DOF), F32),
            vmem((3, RHS, DOF), F32),
            vmem((3, RHS, DOF), F32),
            vmem((2, 1, DOF), F32),
            vmem((total, 1, DOF), F32),
            vmem((64, 1, DOF), F32),
            dma((2 * LOADS + 3,)),
            dma,
            dma((2,)),
            dma,
            dma,
            dma((2, 2)),
            dma((2, CHUNKS)),
            dma,
            dma((2,)),
            dma,
            dma,
            vmem((RHS, DOF), F32),
            dma,
            pltpu.SemaphoreType.REGULAR,
            pltpu.SemaphoreType.REGULAR((4,)),
        ],
        compiler_params=pltpu.CompilerParams(
            collective_id=0, has_side_effects=True, vmem_limit_bytes=60 * 1024 * 1024
        ),
        name="smooth",
    )(source.reshape(NX, RHS, DOF), *blocks, *tops)
    wide = resid.astype(F32)
    update = lifted.astype(F32) + factor * wide
    remainder = wide - factor * image
    return update.reshape(shape), remainder.reshape(shape)


def solution(mesh):
    field = P("ta", "gz", "yx", None, None, None)
    top = P("ta", "gz", "yx", None, None)
    return jax.shard_map(
        body, mesh=mesh, in_specs=(field,) * 7 + (top,) * 4, out_specs=(field, field), check_vma=False
    )
```
